128 devices in a mesh: gx: 4 (over z_hi, core), gy: 4 (over x), band: 8 (over z_lo, y).
Axes of the slice: x: 4, y: 4, z: 4 (z_hi: 2, z_lo: 2; z = z_hi * 2 + z_lo), core: 2. Of those that a mesh axis runs over, the one named last changes fastest.
Arguments:
- orbitals: float32 [64, 32, 32, 384], P('band', 'gx', 'gy'), may hold values from -6 to 6
- potential: float32 [32, 32, 384], P('gx', 'gy'), may hold values from -3 to 0
Outputs:
- filtered: float32 [64, 32, 32, 384], P('band', 'gx', 'gy')
- margin: float32 [64, 64], P('band')
- hamiltonian: float32 [64, 64], P('band')
The draws below stay inside these ranges and needn't reach their ends.
All inputs are finite; a program needn't handle non-finite values.
Results may differ from the reference program's by a relative error of at most 0.000086.
Values sent between devices are 32-bit elements; how exact they have to be, the bound alone decides.
No kernel may reach another device: no remote copies, remote signals or barrier semaphores. Data moves between devices by JAX's collectives and lax.ppermute only.
A program may use at most 128 MiB of HBM per device.

```python
import jax
import jax.numpy as jnp
from jax import lax

NORB = 64
DEGREE = 4
CX = 8
CY = 8
NZ = 384
NX = 32
NY = 32


def levels(stream_key, extent, cuts, low, high):
    def one(position, shards_of):
        draws = jax.random.uniform(jax.random.fold_in(jax.random.fold_in(stream_key, 6), position), (shards_of,), jnp.float32, low / len(cuts), high / len(cuts))
        return jnp.repeat(jnp.exp(draws), extent[position] // shards_of).reshape((-1,) + (1,) * (len(extent) - position - 1))

    factor_of = one(*cuts[0])
    for cut in cuts[1:]:
        factor_of = factor_of * one(*cut)
    return factor_of


def gaussian(key, shape, scale, limit, cuts=(), held_as=jnp.bfloat16):
    loudness = levels(key, shape, cuts, -0.22, 0.18) if cuts else 1.0
    entries = jax.random.normal(key, shape, jnp.float32) * scale * loudness
    return jnp.minimum(jnp.maximum(entries, -limit), limit).astype(held_as)


def setup_inputs(seed: int = 0) -> dict:
    streams_of = jax.random.split(jax.random.key(seed), 3)
    orbitals = gaussian(streams_of[0], (NORB, NX, NY, NZ), 1.0, 6.0, ((0, 8), (1, 4), (2, 4)), jnp.float32)
    potential = jnp.clip(-3.0 + 3.0 * jax.random.uniform(streams_of[1], (NX, NY, NZ), jnp.float32) ** levels(streams_of[1], (NX, NY, NZ), ((0, 4), (1, 4)), -0.2, 0.2), -3.0, 0.0)
    return dict(orbitals=orbitals, potential=potential)


STENCIL_WEIGHTS = (-5369.0 / 1800.0, 12.0 / 7.0, -15.0 / 56.0, 10.0 / 189.0, -1.0 / 112.0, 2.0 / 1925.0, -1.0 / 16632.0)
GRID_SPACING = 0.5
FILTER_CENTER = 24.0
FILTER_HALFWIDTH = 20.0


def hamiltonian_apply(field, potential):
    laplacian = (3.0 * STENCIL_WEIGHTS[0]) * field
    for reach in range(1, 7):
        along_x = jnp.roll(field, reach, 0) + jnp.roll(field, -reach, 0)
        along_y = jnp.roll(field, reach, 1) + jnp.roll(field, -reach, 1)
        along_z = jnp.roll(field, reach, 2) + jnp.roll(field, -reach, 2)
        laplacian = laplacian + STENCIL_WEIGHTS[reach] * (along_x + along_y + along_z)
    return (-0.5 / (GRID_SPACING * GRID_SPACING)) * laplacian + potential * field


def filter_one(single, potential):
    previous = single
    current = (hamiltonian_apply(single, potential) - FILTER_CENTER * single) / FILTER_HALFWIDTH
    for step in range(DEGREE - 1):
        following = 2.0 * (hamiltonian_apply(current, potential) - FILTER_CENTER * current) / FILTER_HALFWIDTH - previous
        previous, current = current, following
    return current, hamiltonian_apply(current, potential)


def reference(orbitals, potential):
    filtered, applied = lax.map(lambda single: filter_one(single, potential), orbitals)
    flat = filtered.reshape(NORB, -1)
    applied_flat = applied.reshape(NORB, -1)
    dims = (((1,), (1,)), ((), ()))
    scale = 1.0 / (CX * CY * NZ)
    margin = lax.dot_general(flat, flat, dims, precision=lax.Precision.HIGHEST, preferred_element_type=jnp.float32) * scale
    hamiltonian = lax.dot_general(flat, applied_flat, dims, precision=lax.Precision.HIGHEST, preferred_element_type=jnp.float32) * scale
    return filtered, margin, hamiltonian
```

```python
import functools

import jax
import jax.numpy as jnp
import ml_dtypes
import numpy as np
from jax import lax
from jax.experimental import pallas as pl
from jax.experimental.pallas import tpu as pltpu
from jax.sharding import PartitionSpec as P

DEGREE = 4

STENCIL_WEIGHTS = (
    -5369.0 / 1800.0,
    12.0 / 7.0,
    -15.0 / 56.0,
    10.0 / 189.0,
    -1.0 / 112.0,
    2.0 / 1925.0,
    -1.0 / 16632.0,
)
GRID_SPACING = 0.5
FILTER_CENTER = 24.0
FILTER_HALFWIDTH = 20.0
KINETIC = -0.5 / (GRID_SPACING * GRID_SPACING)
GRID_AXES = ("gx", "gy")
ALL_AXES = ("band", "gx", "gy")
LANES = 128
HALO = 8
VMEM = pl.BlockSpec(memory_space=pltpu.VMEM)
PARAMS = pltpu.CompilerParams(vmem_limit_bytes=48 * 1024 * 1024)


def lane_index(rows):
    return lax.broadcasted_iota(jnp.int32, (rows, LANES), 1)


def pack_kernel(orb_ref, pot_ref, out_ref):
    lane = lane_index(64)

    def windows(block):
        z0, z1, z2 = (block[:, :, i * LANES : (i + 1) * LANES].reshape(64, LANES) for i in range(3))
        return (
            (z0, jnp.where(lane < 96, z1, z2)),
            (z2, jnp.where(lane < 32, z0, z1)),
        )

    pot = windows(pot_ref[...])
    for j in range(8):
        orb = windows(orb_ref[j])
        for half in range(2):
            for part in range(2):
                out_ref[half * 8 + j, part] = orb[half][part]
                out_ref[half * 8 + j, 2 + part] = pot[half][part]


def band_matrices():
    def circulant(count):
        matrix = np.zeros((count, count), np.float64)
        for reach in range(1, 7):
            for cell in range(count):
                weight = STENCIL_WEIGHTS[reach] / STENCIL_WEIGHTS[1]
                matrix[cell, (cell + reach) % count] += weight
                matrix[cell, (cell - reach) % count] += weight
        return matrix

    def split(matrix):
        high = matrix.astype(ml_dtypes.bfloat16)
        low = (matrix - high.astype(np.float64)).astype(ml_dtypes.bfloat16)
        return high, low

    along_z = split(circulant(256))
    along_y = split(np.kron(np.eye(8), circulant(32)))
    return np.stack(along_z + along_y)


def filter_kernel(half_ref, recv_ref, mat_ref, pack_ref, gram_ref, field_ref, pot_ref):
    half = half_ref[0]
    for gx in range(4):
        for gy in range(4):
            src = gx * 4 + gy
            xs = slice(gx * 8, gx * 8 + 8)
            ys = slice(gy * 8, gy * 8 + 8)
            for part in range(2):
                zs = slice(part * LANES, (part + 1) * LANES)
                piece = recv_ref[src, part].reshape(8, 8, LANES)
                field_ref[0, HALO + gx * 8 : HALO + gx * 8 + 8, ys, zs] = piece
                pot_ref[xs, ys, zs] = recv_ref[src, 2 + part].reshape(8, 8, LANES)

    def wrap(slot):
        field_ref[slot, 0:HALO] = field_ref[slot, 32 : 32 + HALO]
        field_ref[slot, 32 + HALO : 32 + 2 * HALO] = field_ref[slot, HALO : 2 * HALO]

    def apply_group(slot, g):
        x0 = HALO + g * 8
        center = field_ref[slot, pl.ds(x0, 8)]
        flat = center.reshape(256, 256)
        high = flat.astype(jnp.bfloat16)
        low = (flat - high.astype(jnp.float32)).astype(jnp.bfloat16)
        dot = functools.partial(jnp.dot, preferred_element_type=jnp.float32)
        shifts = dot(high, mat_ref[0]) + dot(low, mat_ref[0]) + dot(high, mat_ref[1])
        shifts = shifts + (dot(mat_ref[2], high) + dot(mat_ref[2], low) + dot(mat_ref[3], high))
        shifts = shifts.reshape(8, 32, 256)
        total = (3.0 * STENCIL_WEIGHTS[0] * KINETIC) * center + (
            STENCIL_WEIGHTS[1] * KINETIC
        ) * shifts
        for reach in range(1, 7):
            pair = field_ref[slot, pl.ds(x0 + reach, 8)] + field_ref[slot, pl.ds(x0 - reach, 8)]
            total = total + (STENCIL_WEIGHTS[reach] * KINETIC) * pair
        total = total + pot_ref[pl.ds(g * 8, 8)] * center
        return total, center

    for step in range(DEGREE):
        slot, other = step % 2, (step + 1) % 2
        wrap(slot)

        def advance(g, carry, step=step, slot=slot, other=other):
            applied, center = apply_group(slot, g)
            rows = pl.ds(HALO + g * 8, 8)
            if step == 0:
                following = (applied - FILTER_CENTER * center) * (1.0 / FILTER_HALFWIDTH)
            else:
                following = (applied - FILTER_CENTER * center) * (
                    2.0 / FILTER_HALFWIDTH
                ) - field_ref[other, rows]
            field_ref[other, rows] = following
            return carry

        lax.fori_loop(0, 4, advance, 0)

    slot = DEGREE % 2
    wrap(slot)
    own32 = (lane_index(32) < 64) == (half == 0)
    own8 = ((lax.broadcasted_iota(jnp.int32, (32, 8, LANES), 2) < 64)) == (half == 0)

    def finish(g, carry):
        applied, center = apply_group(slot, g)
        for gy in range(4):
            ys = slice(gy * 8, gy * 8 + 8)
            main = center[:, ys, :LANES].reshape(64, LANES)
            rest = center[:, ys, LANES:].reshape(64, LANES)
            joined = jnp.where(own32, rest[:32], pltpu.roll(rest[32:], 64, 1))
            pack_ref[g * 4 + gy, :64] = main
            pack_ref[g * 4 + gy, 64:] = joined
        tiles = center.reshape(32, 8, 256)
        applied_tiles = applied.reshape(32, 8, 256)
        moved = pltpu.roll(applied_tiles[:, :, LANES:].reshape(256, LANES), 64, 1).reshape(32, 8, LANES)
        rows = pl.ds(g * 32, 32)
        gram_ref[rows, 0:8] = tiles[:, :, :LANES]
        gram_ref[rows, 8:16] = applied_tiles[:, :, :LANES]
        gram_ref[rows, 16:24] = jnp.where(own8, tiles[:, :, LANES:], moved)
        return carry

    lax.fori_loop(0, 4, finish, 0)


def unpack_kernel(recv_ref, out_ref):
    lane = lane_index(32)
    for j in range(8):
        zero, one = recv_ref[j], recv_ref[8 + j]
        out_ref[j, :, :, :LANES] = zero[:64].reshape(8, 8, LANES)
        out_ref[j, :, :, 2 * LANES :] = one[:64].reshape(8, 8, LANES)
        first = jnp.where(lane < 64, zero[64:], one[64:])
        second = pltpu.roll(jnp.where(lane < 64, one[64:], zero[64:]), 64, 1)
        out_ref[j, :4, :, LANES : 2 * LANES] = first.reshape(4, 8, LANES)
        out_ref[j, 4:, :, LANES : 2 * LANES] = second.reshape(4, 8, LANES)


def gram_kernel(recv_ref, out_ref):
    lane = lane_index(64)

    def rows_of(half, k):
        parts = [recv_ref[pl.ds((b * 2 + half) * 8 * 24 + k, 8, stride=24), :] for b in range(8)]
        return jnp.concatenate(parts, axis=0)

    def split(pieces):
        whole = jnp.concatenate(pieces, axis=1)
        high = whole.astype(jnp.bfloat16)
        low = (whole - high.astype(jnp.float32)).astype(jnp.bfloat16)
        return high, low

    total = jnp.zeros((128, 256), jnp.float32)
    for k in range(8):
        rest0, rest1 = rows_of(0, 16 + k), rows_of(1, 16 + k)
        rest = jnp.where(lane < 64, rest0, rest1)
        rest_applied = pltpu.roll(jnp.where(lane < 64, rest1, rest0), 64, 1)
        f1, f2 = split([rows_of(0, k), rows_of(1, k), rest])
        a1, a2 = split([rows_of(0, 8 + k), rows_of(1, 8 + k), rest_applied])
        total = total + lax.dot_general(
            jnp.concatenate([f1, f2], axis=0),
            jnp.concatenate([f1, a1, f2, a2], axis=0),
            (((1,), (1,)), ((), ())),
            preferred_element_type=jnp.float32,
        )
    total = total[:64] + total[64:]
    total = total[:, :LANES] + total[:, LANES:]
    for b in range(8):
        rows = total[b * 8 : b * 8 + 8]
        out_ref[b] = jnp.broadcast_to(rows[None], (16, 8, LANES))


def sum_kernel(recv_ref, margin_ref, hamiltonian_ref, *, scale):
    total = jnp.sum(recv_ref[...], axis=0) * scale
    margin_ref[...] = total[:, :64]
    hamiltonian_ref[...] = pltpu.roll(total, 64, 1)[:, :64]


def call(kernel, shapes, *args, scratch=(), smem=0):
    single = not isinstance(shapes, list)
    outs = [jax.ShapeDtypeStruct(s, jnp.float32) for s in ([shapes] if single else shapes)]
    specs = [pl.BlockSpec(memory_space=pltpu.SMEM)] * smem + [VMEM] * (len(args) - smem)
    result = pl.pallas_call(
        kernel,
        out_shape=outs[0] if single else outs,
        in_specs=specs,
        out_specs=VMEM if single else [VMEM] * len(outs),
        scratch_shapes=list(scratch),
        compiler_params=PARAMS,
    )(*args)
    return result


def exchange(array, axes):
    return lax.all_to_all(array, axes, split_axis=0, concat_axis=0, tiled=True)


def per_device(orbitals, potential):
    packed = call(pack_kernel, (16, 4, 64, LANES), orbitals, potential)
    windows = exchange(packed, GRID_AXES)
    half = (lax.axis_index("gx") // 2).astype(jnp.int32).reshape(1)
    matrices = jnp.asarray(band_matrices())
    pieces, gram_pieces = call(
        filter_kernel,
        [(16, 96, LANES), (128, 24, LANES)],
        half,
        windows,
        matrices,
        scratch=(
            pltpu.VMEM((2, 32 + 2 * HALO, 32, 256), jnp.float32),
            pltpu.VMEM((32, 32, 256), jnp.float32),
        ),
        smem=1,
    )
    gram_cells = exchange(gram_pieces, ALL_AXES)
    partial = call(gram_kernel, (8, 16, 8, LANES), gram_cells.reshape(128 * 24, LANES))
    filtered = call(unpack_kernel, (8, 8, 8, 384), exchange(pieces, GRID_AXES))
    sums = exchange(partial.reshape(128, 8, LANES), ALL_AXES)
    scale = 1.0 / (8 * 8 * 384)
    margin, hamiltonian = call(
        functools.partial(sum_kernel, scale=scale), [(8, 64), (8, 64)], sums
    )
    return filtered, margin, hamiltonian


def solution(mesh):
    placed = (P("band", "gx", "gy", None), P("gx", "gy", None))
    return jax.shard_map(
        per_device,
        mesh=mesh,
        in_specs=placed,
        out_specs=(P("band", "gx", "gy", None), P("band", None), P("band", None)),
        check_vma=False,
    )
```

```python
import functools

import jax
import jax.numpy as jnp
import ml_dtypes
import numpy as np
from jax import lax
from jax.experimental import pallas as pl
from jax.experimental.pallas import tpu as pltpu
from jax.sharding import PartitionSpec as P

DEGREE = 4

STENCIL_WEIGHTS = (
    -5369.0 / 1800.0,
    12.0 / 7.0,
    -15.0 / 56.0,
    10.0 / 189.0,
    -1.0 / 112.0,
    2.0 / 1925.0,
    -1.0 / 16632.0,
)
GRID_SPACING = 0.5
FILTER_CENTER = 24.0
FILTER_HALFWIDTH = 20.0
KINETIC = -0.5 / (GRID_SPACING * GRID_SPACING)
GRID_AXES = ("gx", "gy")
ALL_AXES = ("band", "gx", "gy")
LANES = 128
HALO = 8
VMEM = pl.BlockSpec(memory_space=pltpu.VMEM)
PARAMS = pltpu.CompilerParams(vmem_limit_bytes=48 * 1024 * 1024)


def lane_index(rows):
    return lax.broadcasted_iota(jnp.int32, (rows, LANES), 1)


def pack_kernel(orb_ref, pot_ref, out_ref):
    lane = lane_index(64)

    def windows(block):
        z0, z1, z2 = (block[:, :, i * LANES : (i + 1) * LANES].reshape(64, LANES) for i in range(3))
        return (
            (z0, jnp.where(lane < 96, z1, z2)),
            (z2, jnp.where(lane < 32, z0, z1)),
        )

    pot = windows(pot_ref[...])
    for j in range(8):
        orb = windows(orb_ref[j])
        for half in range(2):
            for part in range(2):
                out_ref[half * 8 + j, part] = orb[half][part]
                out_ref[half * 8 + j, 2 + part] = pot[half][part]


def band_matrices():
    def circulant(count):
        matrix = np.zeros((count, count), np.float64)
        for reach in range(1, 7):
            for cell in range(count):
                weight = STENCIL_WEIGHTS[reach] / STENCIL_WEIGHTS[1]
                matrix[cell, (cell + reach) % count] += weight
                matrix[cell, (cell - reach) % count] += weight
        return matrix

    def split(matrix):
        high = matrix.astype(ml_dtypes.bfloat16)
        low = (matrix - high.astype(np.float64)).astype(ml_dtypes.bfloat16)
        return high, low

    along_z = split(circulant(256))
    along_y = split(np.kron(np.eye(8), circulant(32)))
    return np.stack(along_z + along_y)


def filter_kernel(half_ref, recv_ref, mat_ref, gram_ref, field_ref, pot_ref):
    half = half_ref[0]
    for gx in range(4):
        for gy in range(4):
            src = gx * 4 + gy
            xs = slice(gx * 8, gx * 8 + 8)
            ys = slice(gy * 8, gy * 8 + 8)
            for part in range(2):
                zs = slice(part * LANES, (part + 1) * LANES)
                piece = recv_ref[src, part].reshape(8, 8, LANES)
                field_ref[0, HALO + gx * 8 : HALO + gx * 8 + 8, ys, zs] = piece
                pot_ref[xs, ys, zs] = recv_ref[src, 2 + part].reshape(8, 8, LANES)

    def wrap(slot):
        field_ref[slot, 0:HALO] = field_ref[slot, 32 : 32 + HALO]
        field_ref[slot, 32 + HALO : 32 + 2 * HALO] = field_ref[slot, HALO : 2 * HALO]

    def apply_group(slot, g):
        x0 = HALO + g * 8
        center = field_ref[slot, pl.ds(x0, 8)]
        flat = center.reshape(256, 256)
        high = flat.astype(jnp.bfloat16)
        low = (flat - high.astype(jnp.float32)).astype(jnp.bfloat16)
        dot = functools.partial(jnp.dot, preferred_element_type=jnp.float32)
        shifts = dot(high, mat_ref[0]) + dot(low, mat_ref[0]) + dot(high, mat_ref[1])
        shifts = shifts + (dot(mat_ref[2], high) + dot(mat_ref[2], low) + dot(mat_ref[3], high))
        shifts = shifts.reshape(8, 32, 256)
        total = (3.0 * STENCIL_WEIGHTS[0] * KINETIC) * center + (
            STENCIL_WEIGHTS[1] * KINETIC
        ) * shifts
        for reach in range(1, 7):
            pair = field_ref[slot, pl.ds(x0 + reach, 8)] + field_ref[slot, pl.ds(x0 - reach, 8)]
            total = total + (STENCIL_WEIGHTS[reach] * KINETIC) * pair
        total = total + pot_ref[pl.ds(g * 8, 8)] * center
        return total, center

    for step in range(DEGREE):
        slot, other = step % 2, (step + 1) % 2
        wrap(slot)

        def advance(g, carry, step=step, slot=slot, other=other):
            applied, center = apply_group(slot, g)
            rows = pl.ds(HALO + g * 8, 8)
            if step == 0:
                following = (applied - FILTER_CENTER * center) * (1.0 / FILTER_HALFWIDTH)
            else:
                following = (applied - FILTER_CENTER * center) * (
                    2.0 / FILTER_HALFWIDTH
                ) - field_ref[other, rows]
            field_ref[other, rows] = following
            return carry

        lax.fori_loop(0, 4, advance, 0)

    slot = DEGREE % 2
    wrap(slot)
    own = (lax.broadcasted_iota(jnp.int32, (8, 4, 8, LANES), 3) < 64) == (half == 0)

    def finish(g, carry):
        applied, center = apply_group(slot, g)
        tiles = center.reshape(8, 4, 8, 256)
        applied_tiles = applied.reshape(8, 4, 8, 256)
        moved = pltpu.roll(applied_tiles[..., LANES:].reshape(256, LANES), 64, 1)
        gram_ref[:, g, :, 0:8] = tiles[..., :LANES]
        gram_ref[:, g, :, 8:16] = applied_tiles[..., :LANES]
        gram_ref[:, g, :, 16:24] = jnp.where(
            own, tiles[..., LANES:], moved.reshape(8, 4, 8, LANES)
        )
        return carry

    lax.fori_loop(0, 4, finish, 0)


def gram_kernel(recv_ref, out_ref):
    lane = lane_index(64)

    def rows_of(half, k):
        parts = [recv_ref[pl.ds((b * 2 + half) * 8 * 24 + k, 8, stride=24), :] for b in range(8)]
        return jnp.concatenate(parts, axis=0)

    def split(pieces):
        whole = jnp.concatenate(pieces, axis=1)
        high = whole.astype(jnp.bfloat16)
        low = (whole - high.astype(jnp.float32)).astype(jnp.bfloat16)
        return high, low

    total = jnp.zeros((128, 256), jnp.float32)
    for k in range(8):
        rest0, rest1 = rows_of(0, 16 + k), rows_of(1, 16 + k)
        rest = jnp.where(lane < 64, rest0, rest1)
        rest_applied = pltpu.roll(jnp.where(lane < 64, rest1, rest0), 64, 1)
        f1, f2 = split([rows_of(0, k), rows_of(1, k), rest])
        a1, a2 = split([rows_of(0, 8 + k), rows_of(1, 8 + k), rest_applied])
        total = total + lax.dot_general(
            jnp.concatenate([f1, f2], axis=0),
            jnp.concatenate([f1, a1, f2, a2], axis=0),
            (((1,), (1,)), ((), ())),
            preferred_element_type=jnp.float32,
        )
    total = total[:64] + total[64:]
    total = total[:, :LANES] + total[:, LANES:]
    near = lane_index(8) < 64
    for b in range(8):
        for j in range(8):
            zero, one = (((b * 2 + h) * 8 + j) * 24 for h in range(2))
            rest = jnp.where(near, recv_ref[zero + 16 : zero + 24], recv_ref[one + 16 : one + 24])
            out_ref[b, j * 8 : j * 8 + 8] = recv_ref[zero : zero + 8]
            out_ref[b, 64 + j * 8 : 64 + j * 8 + 8] = rest
            out_ref[b, 128 + j * 8 : 128 + j * 8 + 8] = recv_ref[one : one + 8]
        out_ref[b, 192:200] = total[b * 8 : b * 8 + 8]


def band_sum_kernel(recv_ref, out_ref):
    total = jnp.sum(recv_ref[:, 192:200], axis=0)
    out_ref[...] = jnp.broadcast_to(total[None], (16, 8, LANES))


def unpack_kernel(recv_ref, out_ref):
    for x in range(8):
        for part in range(3):
            piece = recv_ref[x, part * 64 : part * 64 + 64].reshape(8, 8, LANES)
            out_ref[:, x, :, part * LANES : (part + 1) * LANES] = piece


def sum_kernel(recv_ref, margin_ref, hamiltonian_ref, *, scale):
    total = jnp.sum(recv_ref[...], axis=0) * scale
    margin_ref[...] = total[:, :64]
    hamiltonian_ref[...] = pltpu.roll(total, 64, 1)[:, :64]


def call(kernel, shapes, *args, scratch=(), smem=0):
    single = not isinstance(shapes, list)
    outs = [jax.ShapeDtypeStruct(s, jnp.float32) for s in ([shapes] if single else shapes)]
    specs = [pl.BlockSpec(memory_space=pltpu.SMEM)] * smem + [VMEM] * (len(args) - smem)
    result = pl.pallas_call(
        kernel,
        out_shape=outs[0] if single else outs,
        in_specs=specs,
        out_specs=VMEM if single else [VMEM] * len(outs),
        scratch_shapes=list(scratch),
        compiler_params=PARAMS,
    )(*args)
    return result


def exchange(array, axes):
    return lax.all_to_all(array, axes, split_axis=0, concat_axis=0, tiled=True)


def per_device(orbitals, potential):
    packed = call(pack_kernel, (16, 4, 64, LANES), orbitals, potential)
    windows = exchange(packed, GRID_AXES)
    half = (lax.axis_index("gx") // 2).astype(jnp.int32).reshape(1)
    matrices = jnp.asarray(band_matrices())
    rows = call(
        filter_kernel,
        (8, 4, 4, 24, LANES),
        half,
        windows,
        matrices,
        scratch=(
            pltpu.VMEM((2, 32 + 2 * HALO, 32, 256), jnp.float32),
            pltpu.VMEM((32, 32, 256), jnp.float32),
        ),
        smem=1,
    )
    cells = exchange(rows.reshape(128, 24, LANES), ALL_AXES)
    outgoing = call(gram_kernel, (8, 200, LANES), cells.reshape(128 * 24, LANES))
    home = exchange(outgoing, "band")
    sums = exchange(call(band_sum_kernel, (16, 8, LANES), home), GRID_AXES)
    filtered = call(unpack_kernel, (8, 8, 8, 384), home)
    scale = 1.0 / (8 * 8 * 384)
    margin, hamiltonian = call(
        functools.partial(sum_kernel, scale=scale), [(8, 64), (8, 64)], sums
    )
    return filtered, margin, hamiltonian


def solution(mesh):
    placed = (P("band", "gx", "gy", None), P("gx", "gy", None))
    return jax.shard_map(
        per_device,
        mesh=mesh,
        in_specs=placed,
        out_specs=(P("band", "gx", "gy", None), P("band", None), P("band", None)),
        check_vma=False,
    )
```

```python
import functools

import jax
import jax.numpy as jnp
import ml_dtypes
import numpy as np
from jax import lax
from jax.experimental import pallas as pl
from jax.experimental.pallas import tpu as pltpu
from jax.sharding import PartitionSpec as P

DEGREE = 4

STENCIL_WEIGHTS = (
    -5369.0 / 1800.0,
    12.0 / 7.0,
    -15.0 / 56.0,
    10.0 / 189.0,
    -1.0 / 112.0,
    2.0 / 1925.0,
    -1.0 / 16632.0,
)
GRID_SPACING = 0.5
FILTER_CENTER = 24.0
FILTER_HALFWIDTH = 20.0
KINETIC = -0.5 / (GRID_SPACING * GRID_SPACING)
STEP = 2.0 / FILTER_HALFWIDTH
GRID_AXES = ("gx", "gy")
ALL_AXES = ("band", "gx", "gy")
LANES = 128
HALO = 8
VMEM = pl.BlockSpec(memory_space=pltpu.VMEM)
PARAMS = pltpu.CompilerParams(vmem_limit_bytes=48 * 1024 * 1024)


def lane_index(rows):
    return lax.broadcasted_iota(jnp.int32, (rows, LANES), 1)


def pack_kernel(orb_ref, pot_ref, out_ref, orb, pot, packed, in_sems, out_sems):
    loads = [pltpu.make_async_copy(pot_ref, pot, in_sems.at[8])]
    loads += [pltpu.make_async_copy(orb_ref.at[j], orb.at[j], in_sems.at[j]) for j in range(8)]
    for load in loads:
        load.start()
    lane = lane_index(64)

    def windows(block):
        z0, z1, z2 = (block[:, :, i * LANES : (i + 1) * LANES].reshape(64, LANES) for i in range(3))
        return (
            (z0, jnp.where(lane < 96, z1, z2)),
            (z2, jnp.where(lane < 32, z0, z1)),
        )

    loads[0].wait()
    pot_windows = windows(pot[...])
    for half in range(2):
        for j in range(8):
            packed[half, j, 2] = pot_windows[half][j // 4]
    stores = []
    for j in range(8):
        loads[1 + j].wait()
        orb_windows = windows(orb[j])
        for half in range(2):
            for part in range(2):
                packed[half, j, part] = orb_windows[half][part]
        stores.append(
            pltpu.make_async_copy(packed.at[:, j], out_ref.at[:, j], out_sems.at[j])
        )
        stores[-1].start()
    for store in stores:
        store.wait()


def band_matrices():
    def circulant(count):
        matrix = np.zeros((count, count), np.float64)
        for reach in range(1, 7):
            for cell in range(count):
                weight = STENCIL_WEIGHTS[reach] / STENCIL_WEIGHTS[1]
                matrix[cell, (cell + reach) % count] += weight
                matrix[cell, (cell - reach) % count] += weight
        return matrix

    def split(matrix):
        high = matrix.astype(ml_dtypes.bfloat16)
        low = (matrix - high.astype(np.float64)).astype(ml_dtypes.bfloat16)
        return high, low

    z_high, z_low = split(circulant(256))
    y_high, y_low = split(np.kron(np.eye(8), circulant(32)))
    return np.concatenate([z_high, z_high, z_low]), np.concatenate(
        [y_high[:128, :128], y_high[:128, :128]], axis=1
    ), y_low


def kinetic_group(field_ref, mats, g):
    z_ref, y_ref, y_low_ref = mats
    x0 = HALO + g * 8
    center = field_ref[x0 : x0 + 8]
    flat = center.reshape(256, 256)
    high = flat.astype(jnp.bfloat16)
    low = (flat - high.astype(jnp.float32)).astype(jnp.bfloat16)
    dot = functools.partial(jnp.dot, preferred_element_type=jnp.float32)
    shifts = dot(jnp.concatenate([high, low, high], axis=1), z_ref[...])
    along_y = [
        dot(y_ref[...], jnp.concatenate([high[rows], low[rows]], axis=0))
        for rows in (slice(0, 128), slice(128, 256))
    ]
    shifts = shifts + jnp.concatenate(along_y, axis=0) + dot(y_low_ref[...], high)
    total = (STENCIL_WEIGHTS[1] * KINETIC * STEP) * shifts.reshape(8, 32, 256)
    for reach in range(1, 7):
        pair = field_ref[x0 + reach : x0 + reach + 8] + field_ref[x0 - reach : x0 - reach + 8]
        total = total + (STENCIL_WEIGHTS[reach] * KINETIC * STEP) * pair
    return total, center


def wrap(field_ref):
    field_ref[0:HALO] = field_ref[32 : 32 + HALO]
    field_ref[32 + HALO : 32 + 2 * HALO] = field_ref[HALO : 2 * HALO]


def domain(gx, gy):
    return gx * 4 + gy, slice(gx * 8, gx * 8 + 8), slice(gy * 8, gy * 8 + 8)


def kinetic_kernel(recv_ref, z_ref, y_ref, y_low_ref, out_ref, field_ref):
    for gx in range(4):
        for gy in range(4):
            src, xs, ys = domain(gx, gy)
            for part in range(2):
                piece = recv_ref[src, part].reshape(8, 8, LANES)
                zs = slice(part * LANES, (part + 1) * LANES)
                field_ref[HALO + gx * 8 : HALO + gx * 8 + 8, ys, zs] = piece
    wrap(field_ref)
    for g in range(4):
        out_ref[g * 8 : g * 8 + 8], _ = kinetic_group(field_ref, (z_ref, y_ref, y_low_ref), g)


def filter_kernel(
    place_ref, recv_ref, other_ref, first_ref, z_ref, y_ref, y_low_ref, out_ref, even_ref, odd_ref, pot_ref
):
    half, core = place_ref[0], place_ref[1]
    mats = (z_ref, y_ref, y_low_ref)
    for gx in range(4):
        for gy in range(4):
            src, xs, ys = domain(gx, gy)
            mine = recv_ref[src, 2]
            theirs = other_ref[src]
            rows = slice(HALO + gx * 8, HALO + gx * 8 + 8)
            for part in range(2):
                zs = slice(part * LANES, (part + 1) * LANES)
                tile = jnp.where(core == part, mine, theirs).reshape(8, 8, LANES)
                local = (tile + (3.0 * STENCIL_WEIGHTS[0] * KINETIC - FILTER_CENTER)) * STEP
                pot_ref[xs, ys, zs] = local
                start = recv_ref[src, part].reshape(8, 8, LANES)
                even_ref[rows, ys, zs] = start
                odd_ref[rows, ys, zs] = 0.5 * (first_ref[xs, ys, zs] + local * start)

    def apply_group(field_ref, g):
        total, center = kinetic_group(field_ref, mats, g)
        return total + pot_ref[g * 8 : g * 8 + 8] * center, center

    for step in range(1, DEGREE):
        current, previous = (odd_ref, even_ref) if step % 2 else (even_ref, odd_ref)
        wrap(current)
        for g in range(4):
            total, _ = apply_group(current, g)
            rows = slice(HALO + g * 8, HALO + g * 8 + 8)
            previous[rows] = total - previous[rows]

    last = odd_ref if DEGREE % 2 else even_ref
    wrap(last)
    own = (lax.broadcasted_iota(jnp.int32, (8, 4, 8, LANES), 3) < 64) == (half == 0)
    for g in range(4):
        total, center = apply_group(last, g)
        applied = total * (1.0 / STEP) + FILTER_CENTER * center
        tiles = center.reshape(8, 4, 8, 256)
        applied_tiles = applied.reshape(8, 4, 8, 256)
        moved = pltpu.roll(applied_tiles[..., LANES:].reshape(256, LANES), 64, 1)
        out_ref[:, g, :, 0:8] = tiles[..., :LANES]
        out_ref[:, g, :, 8:16] = applied_tiles[..., :LANES]
        out_ref[:, g, :, 16:24] = jnp.where(
            own, tiles[..., LANES:], moved.reshape(8, 4, 8, LANES)
        )


def gram_kernel(recv_ref, out_ref):
    lane = lane_index(64)

    def rows_of(half, k):
        parts = [recv_ref[pl.ds((b * 2 + half) * 8 * 24 + k, 8, stride=24), :] for b in range(8)]
        return jnp.concatenate(parts, axis=0)

    def split(pieces):
        whole = jnp.concatenate(pieces, axis=1)
        high = whole.astype(jnp.bfloat16)
        low = (whole - high.astype(jnp.float32)).astype(jnp.bfloat16)
        return high, low

    total = jnp.zeros((128, 256), jnp.float32)
    for k in range(8):
        rest0, rest1 = rows_of(0, 16 + k), rows_of(1, 16 + k)
        rest = jnp.where(lane < 64, rest0, rest1)
        rest_applied = pltpu.roll(jnp.where(lane < 64, rest1, rest0), 64, 1)
        f1, f2 = split([rows_of(0, k), rows_of(1, k), rest])
        a1, a2 = split([rows_of(0, 8 + k), rows_of(1, 8 + k), rest_applied])
        total = total + lax.dot_general(
            jnp.concatenate([f1, f2], axis=0),
            jnp.concatenate([f1, a1, f2, a2], axis=0),
            (((1,), (1,)), ((), ())),
            preferred_element_type=jnp.float32,
        )
    total = total[:64] + total[64:]
    total = total[:, :LANES] + total[:, LANES:]
    near = lane_index(8) < 64
    for b in range(8):
        for j in range(8):
            zero, one = (((b * 2 + h) * 8 + j) * 24 for h in range(2))
            rest = jnp.where(near, recv_ref[zero + 16 : zero + 24], recv_ref[one + 16 : one + 24])
            out_ref[b, j * 8 : j * 8 + 8] = recv_ref[zero : zero + 8]
            out_ref[b, 64 + j * 8 : 64 + j * 8 + 8] = rest
            out_ref[b, 128 + j * 8 : 128 + j * 8 + 8] = recv_ref[one : one + 8]
        out_ref[b, 192:200] = total[b * 8 : b * 8 + 8]


def band_sum_kernel(recv_ref, out_ref):
    total = jnp.sum(recv_ref[:, 192:200], axis=0)
    out_ref[...] = jnp.broadcast_to(total[None], (16, 8, LANES))


def unpack_kernel(recv_ref, out_ref):
    for x in range(8):
        for part in range(3):
            piece = recv_ref[x, part * 64 : part * 64 + 64].reshape(8, 8, LANES)
            out_ref[:, x, :, part * LANES : (part + 1) * LANES] = piece


def sum_kernel(recv_ref, margin_ref, hamiltonian_ref, *, scale):
    total = jnp.sum(recv_ref[...], axis=0) * scale
    margin_ref[...] = total[:, :64]
    hamiltonian_ref[...] = pltpu.roll(total, 64, 1)[:, :64]


def call(kernel, shapes, *args, scratch=(), smem=0):
    single = not isinstance(shapes, list)
    outs = [jax.ShapeDtypeStruct(s, jnp.float32) for s in ([shapes] if single else shapes)]
    specs = [pl.BlockSpec(memory_space=pltpu.SMEM)] * smem + [VMEM] * (len(args) - smem)
    result = pl.pallas_call(
        kernel,
        out_shape=outs[0] if single else outs,
        in_specs=specs,
        out_specs=VMEM if single else [VMEM] * len(outs),
        scratch_shapes=list(scratch),
        compiler_params=PARAMS,
    )(*args)
    return result


def exchange(array, axes):
    return lax.all_to_all(array, axes, split_axis=0, concat_axis=0, tiled=True)


def pack(orbitals, potential):
    hbm = pl.BlockSpec(memory_space=pltpu.HBM)
    return pl.pallas_call(
        pack_kernel,
        out_shape=pltpu.HBM((2, 8, 3, 64, LANES), jnp.float32),
        in_specs=[hbm, hbm],
        out_specs=hbm,
        scratch_shapes=[
            pltpu.VMEM((8, 8, 8, 384), jnp.float32),
            pltpu.VMEM((8, 8, 384), jnp.float32),
            pltpu.VMEM((2, 8, 3, 64, LANES), jnp.float32),
            pltpu.SemaphoreType.DMA((9,)),
            pltpu.SemaphoreType.DMA((8,)),
        ],
        compiler_params=PARAMS,
    )(*(pltpu.with_memory_space_constraint(a, pltpu.HBM) for a in (orbitals, potential)))


def per_device(orbitals, potential):
    packed = pack(orbitals, potential).reshape(16, 3, 64, LANES)
    windows = exchange(packed, GRID_AXES)
    other = lax.ppermute(windows[:, 2], "gx", [(0, 1), (1, 0), (2, 3), (3, 2)])
    place = lax.axis_index("gx")
    place = jnp.stack([place // 2, place % 2]).astype(jnp.int32)
    matrices = [jnp.asarray(m) for m in band_matrices()]
    padded = pltpu.VMEM((32 + 2 * HALO, 32, 256), jnp.float32)
    whole = pltpu.VMEM((32, 32, 256), jnp.float32)
    first = call(kinetic_kernel, (32, 32, 256), windows, *matrices, scratch=(padded,))
    rows = call(
        filter_kernel,
        (8, 4, 4, 24, LANES),
        place,
        windows,
        other,
        first,
        *matrices,
        scratch=(padded, padded, whole),
        smem=1,
    )
    cells = exchange(rows.reshape(128, 24, LANES), ALL_AXES)
    outgoing = call(gram_kernel, (8, 200, LANES), cells.reshape(128 * 24, LANES))
    home = exchange(outgoing, "band")
    sums = exchange(call(band_sum_kernel, (16, 8, LANES), home), GRID_AXES)
    filtered = call(unpack_kernel, (8, 8, 8, 384), home)
    scale = 1.0 / (8 * 8 * 384)
    margin, hamiltonian = call(
        functools.partial(sum_kernel, scale=scale), [(8, 64), (8, 64)], sums
    )
    return filtered, margin, hamiltonian


def solution(mesh):
    placed = (P("band", "gx", "gy", None), P("gx", "gy", None))
    return jax.shard_map(
        per_device,
        mesh=mesh,
        in_specs=placed,
        out_specs=(P("band", "gx", "gy", None), P("band", None), P("band", None)),
        check_vma=False,
    )
```

```python
import functools

import jax
import jax.numpy as jnp
import ml_dtypes
import numpy as np
from jax import lax
from jax.experimental import pallas as pl
from jax.experimental.pallas import tpu as pltpu
from jax.sharding import PartitionSpec as P

DEGREE = 4

STENCIL_WEIGHTS = (
    -5369.0 / 1800.0,
    12.0 / 7.0,
    -15.0 / 56.0,
    10.0 / 189.0,
    -1.0 / 112.0,
    2.0 / 1925.0,
    -1.0 / 16632.0,
)
GRID_SPACING = 0.5
FILTER_CENTER = 24.0
FILTER_HALFWIDTH = 20.0
KINETIC = -0.5 / (GRID_SPACING * GRID_SPACING)
STEP = 2.0 / FILTER_HALFWIDTH
FIRST = STENCIL_WEIGHTS[1] * KINETIC * STEP
GRID_AXES = ("gx", "gy")
ALL_AXES = ("band", "gx", "gy")
LANES = 128
VMEM = pl.BlockSpec(memory_space=pltpu.VMEM)
PARAMS = pltpu.CompilerParams(vmem_limit_bytes=24 * 1024 * 1024)


def lane_index(rows):
    return lax.broadcasted_iota(jnp.int32, (rows, LANES), 1)


def pack_kernel(orb_ref, pot_ref, mats_ref, out_ref, mats_out_ref, orb, pot, sems):
    loads = [pltpu.make_async_copy(pot_ref, pot, sems.at[8])]
    loads += [pltpu.make_async_copy(orb_ref.at[j], orb.at[j], sems.at[j]) for j in range(8)]
    loads += [pltpu.make_async_copy(mats_ref, mats_out_ref, sems.at[9])]
    for load in loads:
        load.start()
    lane = lane_index(64)

    def windows(block):
        z0, z1, z2 = (block[:, :, i * LANES : (i + 1) * LANES].reshape(64, LANES) for i in range(3))
        return (
            (z0, jnp.where(lane < 96, z1, z2)),
            (z2, jnp.where(lane < 32, z0, z1)),
        )

    loads[0].wait()
    pot_windows = windows(pot[...])
    for half in range(2):
        for j in range(8):
            out_ref[half, j, 2] = pot_windows[half][j // 4]
    for j in range(8):
        loads[1 + j].wait()
        orb_windows = windows(orb[j])
        for half in range(2):
            for part in range(2):
                out_ref[half, j, part] = orb_windows[half][part]
    loads[9].wait()


def band_matrices():
    def circulant(count):
        matrix = np.zeros((count, count), np.float64)
        for reach in range(1, 7):
            for cell in range(count):
                weight = STENCIL_WEIGHTS[reach] / STENCIL_WEIGHTS[1]
                matrix[cell, (cell + reach) % count] += weight
                matrix[cell, (cell - reach) % count] += weight
        return matrix

    def split(matrix):
        high = matrix.astype(ml_dtypes.bfloat16)
        low = (matrix - high.astype(np.float64)).astype(ml_dtypes.bfloat16)
        return high, low

    z_high, z_low = split(circulant(256))
    y_high, y_low = split(np.kron(np.eye(8), circulant(32)))
    x_high, x_low = split(np.kron(circulant(32), np.eye(8)))
    both = np.concatenate([y_high[:128, :128], y_high[:128, :128]], axis=1)
    return np.concatenate([z_high, z_low, x_high, x_low, y_low, both])


Z_HIGH, Z_LOW, X_HIGH, X_LOW, Y_LOW = (slice(i * 256, i * 256 + 256) for i in range(5))
Y_BOTH = slice(5 * 256, 5 * 256 + 128)


def dot(left, right):
    return jnp.dot(left, right, preferred_element_type=jnp.float32)


def split(field):
    high = field.astype(jnp.bfloat16)
    return high, (field - high.astype(jnp.float32)).astype(jnp.bfloat16)


def add_along_x(field_ref, mats, out_ref, start):
    for tile in range(4):
        ys = slice(tile * 8, tile * 8 + 8)
        if tile < 2:
            field = field_ref[:, ys, :]
            high, low = split(field.reshape(256, 256))
            shifts = dot(mats[X_HIGH], high) + dot(mats[X_HIGH], low) + dot(mats[X_LOW], high)
            out_ref[:, ys, :] = start(field, (slice(None), ys, slice(None))) + FIRST * shifts.reshape(
                32, 8, 256
            )
            continue
        for part in range(2):
            zs = slice(part * LANES, (part + 1) * LANES)
            planes = [field_ref[x, ys, zs] for x in range(32)]
            for x in range(32):
                total = start(planes[x], (x, ys, zs))
                for reach in range(1, 7):
                    pair = planes[(x + reach) % 32] + planes[(x - reach) % 32]
                    total = total + (STENCIL_WEIGHTS[reach] * KINETIC * STEP) * pair
                out_ref[x, ys, zs] = total


def along_yz(field_ref, mats, g):
    center = field_ref[g * 8 : g * 8 + 8]
    high, low = split(center.reshape(256, 256))
    shifts = dot(high, mats[Z_HIGH]) + dot(low, mats[Z_HIGH]) + dot(high, mats[Z_LOW])
    along_y = [
        dot(mats[Y_BOTH], jnp.concatenate([high[rows], low[rows]], axis=0))
        for rows in (slice(0, 128), slice(128, 256))
    ]
    shifts = shifts + jnp.concatenate(along_y, axis=0) + dot(mats[Y_LOW], high)
    return FIRST * shifts.reshape(8, 32, 256), center


def domain(gx, gy):
    return gx * 4 + gy, slice(gx * 8, gx * 8 + 8), slice(gy * 8, gy * 8 + 8)


def own_tile_kernel(recv_ref, out_ref):
    out_ref[...] = recv_ref[:, 2]


def kinetic_kernel(recv_ref, mats, out_ref, field_ref):
    for gx in range(4):
        for gy in range(4):
            src, xs, ys = domain(gx, gy)
            for part in range(2):
                zs = slice(part * LANES, (part + 1) * LANES)
                field_ref[xs, ys, zs] = recv_ref[src, part].reshape(8, 8, LANES)
    add_along_x(field_ref, mats, out_ref, lambda field, at: 0.0)
    for g in range(4):
        rows = slice(g * 8, g * 8 + 8)
        out_ref[rows] = out_ref[rows] + along_yz(field_ref, mats, g)[0]


def filter_kernel(
    place_ref, recv_ref, other_ref, first_ref, mats, out_ref, even_ref, odd_ref, pot_ref
):
    half, core = place_ref[0], place_ref[1]
    for gx in range(4):
        for gy in range(4):
            src, xs, ys = domain(gx, gy)
            mine = recv_ref[src, 2]
            theirs = other_ref[src]
            for part in range(2):
                zs = slice(part * LANES, (part + 1) * LANES)
                tile = jnp.where(core == part, mine, theirs).reshape(8, 8, LANES)
                local = (tile + (3.0 * STENCIL_WEIGHTS[0] * KINETIC - FILTER_CENTER)) * STEP
                pot_ref[xs, ys, zs] = local
                start = recv_ref[src, part].reshape(8, 8, LANES)
                even_ref[xs, ys, zs] = start
                odd_ref[xs, ys, zs] = 0.5 * (first_ref[xs, ys, zs] + local * start)

    for step in range(1, DEGREE):
        current, previous = (odd_ref, even_ref) if step % 2 else (even_ref, odd_ref)
        add_along_x(
            current,
            mats,
            previous,
            lambda field, at, previous=previous: pot_ref[at] * field - previous[at],
        )
        for g in range(4):
            rows = slice(g * 8, g * 8 + 8)
            previous[rows] = previous[rows] + along_yz(current, mats, g)[0]

    last, spare = (odd_ref, even_ref) if DEGREE % 2 else (even_ref, odd_ref)
    add_along_x(last, mats, spare, lambda field, at: pot_ref[at] * field)
    own = (lax.broadcasted_iota(jnp.int32, (8, 4, 8, LANES), 3) < 64) == (half == 0)
    for g in range(4):
        shifts, center = along_yz(last, mats, g)
        total = spare[g * 8 : g * 8 + 8] + shifts
        applied = total * (1.0 / STEP) + FILTER_CENTER * center
        tiles = center.reshape(8, 4, 8, 256)
        applied_tiles = applied.reshape(8, 4, 8, 256)
        moved = pltpu.roll(applied_tiles[..., LANES:].reshape(256, LANES), 64, 1)
        out_ref[:, g, :, 0:8] = tiles[..., :LANES]
        out_ref[:, g, :, 8:16] = applied_tiles[..., :LANES]
        out_ref[:, g, :, 16:24] = jnp.where(
            own, tiles[..., LANES:], moved.reshape(8, 4, 8, LANES)
        )


def gram_kernel(recv_ref, out_ref):
    lane = lane_index(64)

    def rows_of(half, k):
        parts = [recv_ref[pl.ds((b * 2 + half) * 8 * 24 + k, 8, stride=24), :] for b in range(8)]
        return jnp.concatenate(parts, axis=0)

    def split(pieces):
        whole = jnp.concatenate(pieces, axis=1)
        high = whole.astype(jnp.bfloat16)
        low = (whole - high.astype(jnp.float32)).astype(jnp.bfloat16)
        return high, low

    total = jnp.zeros((128, 256), jnp.float32)
    for k in range(8):
        rest0, rest1 = rows_of(0, 16 + k), rows_of(1, 16 + k)
        rest = jnp.where(lane < 64, rest0, rest1)
        rest_applied = pltpu.roll(jnp.where(lane < 64, rest1, rest0), 64, 1)
        f1, f2 = split([rows_of(0, k), rows_of(1, k), rest])
        a1, a2 = split([rows_of(0, 8 + k), rows_of(1, 8 + k), rest_applied])
        total = total + lax.dot_general(
            jnp.concatenate([f1, f2], axis=0),
            jnp.concatenate([f1, a1, f2, a2], axis=0),
            (((1,), (1,)), ((), ())),
            preferred_element_type=jnp.float32,
        )
    total = total[:64] + total[64:]
    total = total[:, :LANES] + total[:, LANES:]
    near = lane_index(8) < 64
    for b in range(8):
        for j in range(8):
            zero, one = (((b * 2 + h) * 8 + j) * 24 for h in range(2))
            rest = jnp.where(near, recv_ref[zero + 16 : zero + 24], recv_ref[one + 16 : one + 24])
            out_ref[b, j * 8 : j * 8 + 8] = recv_ref[zero : zero + 8]
            out_ref[b, 64 + j * 8 : 64 + j * 8 + 8] = rest
            out_ref[b, 128 + j * 8 : 128 + j * 8 + 8] = recv_ref[one : one + 8]
        out_ref[b, 192:200] = total[b * 8 : b * 8 + 8]


def band_sum_kernel(recv_ref, out_ref):
    total = jnp.sum(recv_ref[:, 192:200], axis=0)
    out_ref[...] = jnp.broadcast_to(total[None], (16, 8, LANES))


def unpack_kernel(recv_ref, out_ref):
    for x in range(8):
        for part in range(3):
            piece = recv_ref[x, part * 64 : part * 64 + 64].reshape(8, 8, LANES)
            out_ref[:, x, :, part * LANES : (part + 1) * LANES] = piece


def sum_kernel(recv_ref, margin_ref, hamiltonian_ref, *, scale):
    total = jnp.sum(recv_ref[...], axis=0) * scale
    margin_ref[...] = total[:, :64]
    hamiltonian_ref[...] = pltpu.roll(total, 64, 1)[:, :64]


def call(kernel, shapes, *args, scratch=(), smem=0):
    single = not isinstance(shapes, list)
    outs = [jax.ShapeDtypeStruct(s, jnp.float32) for s in ([shapes] if single else shapes)]
    specs = [pl.BlockSpec(memory_space=pltpu.SMEM)] * smem + [VMEM] * (len(args) - smem)
    result = pl.pallas_call(
        kernel,
        out_shape=outs[0] if single else outs,
        in_specs=specs,
        out_specs=VMEM if single else [VMEM] * len(outs),
        scratch_shapes=list(scratch),
        compiler_params=PARAMS,
    )(*args)
    return result


def exchange(array, axes):
    return lax.all_to_all(array, axes, split_axis=0, concat_axis=0, tiled=True)


def pack(orbitals, potential):
    hbm = pl.BlockSpec(memory_space=pltpu.HBM)
    matrices = jnp.asarray(band_matrices())
    args = (orbitals, potential, matrices)
    return pl.pallas_call(
        pack_kernel,
        out_shape=[
            pltpu.VMEM((2, 8, 3, 64, LANES), jnp.float32),
            pltpu.VMEM(matrices.shape, jnp.bfloat16),
        ],
        in_specs=[hbm] * 3,
        out_specs=[VMEM] * 2,
        scratch_shapes=[
            pltpu.VMEM((8, 8, 8, 384), jnp.float32),
            pltpu.VMEM((8, 8, 384), jnp.float32),
            pltpu.SemaphoreType.DMA((10,)),
        ],
        compiler_params=PARAMS,
    )(*(pltpu.with_memory_space_constraint(a, pltpu.HBM) for a in args))


def per_device(orbitals, potential):
    packed, matrices = pack(orbitals, potential)
    windows = exchange(packed.reshape(16, 3, 64, LANES), GRID_AXES)
    mine = pl.pallas_call(
        own_tile_kernel,
        out_shape=pltpu.VMEM((16, 64, LANES), jnp.float32),
        in_specs=[VMEM],
        out_specs=VMEM,
        compiler_params=PARAMS,
    )(windows)
    other = lax.ppermute(mine, "gx", [(0, 1), (1, 0), (2, 3), (3, 2)])
    place = lax.axis_index("gx")
    place = jnp.stack([place // 2, place % 2]).astype(jnp.int32)
    whole = pltpu.VMEM((32, 32, 256), jnp.float32)
    first = call(kinetic_kernel, (32, 32, 256), windows, matrices, scratch=(whole,))
    rows = call(
        filter_kernel,
        (8, 4, 4, 24, LANES),
        place,
        windows,
        other,
        first,
        matrices,
        scratch=(whole, whole, whole),
        smem=1,
    )
    cells = exchange(rows.reshape(128, 24, LANES), ALL_AXES)
    outgoing = call(gram_kernel, (8, 200, LANES), cells.reshape(128 * 24, LANES))
    home = exchange(outgoing, "band")
    sums = exchange(call(band_sum_kernel, (16, 8, LANES), home), GRID_AXES)
    filtered = call(unpack_kernel, (8, 8, 8, 384), home)
    scale = 1.0 / (8 * 8 * 384)
    margin, hamiltonian = call(
        functools.partial(sum_kernel, scale=scale), [(8, 64), (8, 64)], sums
    )
    return filtered, margin, hamiltonian


def solution(mesh):
    placed = (P("band", "gx", "gy", None), P("gx", "gy", None))
    return jax.shard_map(
        per_device,
        mesh=mesh,
        in_specs=placed,
        out_specs=(P("band", "gx", "gy", None), P("band", None), P("band", None)),
        check_vma=False,
    )
```

```python
import functools

import jax
import jax.numpy as jnp
import ml_dtypes
import numpy as np
from jax import lax
from jax.experimental import pallas as pl
from jax.experimental.pallas import tpu as pltpu
from jax.sharding import PartitionSpec as P

DEGREE = 4

STENCIL_WEIGHTS = (
    -5369.0 / 1800.0,
    12.0 / 7.0,
    -15.0 / 56.0,
    10.0 / 189.0,
    -1.0 / 112.0,
    2.0 / 1925.0,
    -1.0 / 16632.0,
)
GRID_SPACING = 0.5
FILTER_CENTER = 24.0
FILTER_HALFWIDTH = 20.0
KINETIC = -0.5 / (GRID_SPACING * GRID_SPACING)
STEP = 2.0 / FILTER_HALFWIDTH
FIRST = STENCIL_WEIGHTS[1] * KINETIC * STEP
GRID_AXES = ("gx", "gy")
ALL_AXES = ("band", "gx", "gy")
LANES = 128
VMEM = pl.BlockSpec(memory_space=pltpu.VMEM)
PARAMS = pltpu.CompilerParams(vmem_limit_bytes=24 * 1024 * 1024)


def lane_index(rows):
    return lax.broadcasted_iota(jnp.int32, (rows, LANES), 1)


def pack_kernel(orb_ref, pot_ref, mats_ref, out_ref, mats_out_ref, orb, pot, sems):
    loads = [pltpu.make_async_copy(pot_ref, pot, sems.at[8])]
    loads += [pltpu.make_async_copy(orb_ref.at[j], orb.at[j], sems.at[j]) for j in range(8)]
    loads += [pltpu.make_async_copy(mats_ref, mats_out_ref, sems.at[9])]
    for load in loads:
        load.start()
    lane = lane_index(64)

    def windows(block):
        z0, z1, z2 = (block[:, :, i * LANES : (i + 1) * LANES].reshape(64, LANES) for i in range(3))
        return (
            (z0, jnp.where(lane < 96, z1, z2)),
            (z2, jnp.where(lane < 32, z0, z1)),
        )

    loads[0].wait()
    pot_windows = windows(pot[...])
    for half in range(2):
        for j in range(8):
            out_ref[half, j, 2] = pot_windows[half][j // 4]
    for j in range(8):
        loads[1 + j].wait()
        orb_windows = windows(orb[j])
        for half in range(2):
            for part in range(2):
                out_ref[half, j, part] = orb_windows[half][part]
    loads[9].wait()


def band_matrices():
    def circulant(count):
        matrix = np.zeros((count, count), np.float64)
        for reach in range(1, 7):
            for cell in range(count):
                weight = STENCIL_WEIGHTS[reach] / STENCIL_WEIGHTS[1]
                matrix[cell, (cell + reach) % count] += weight
                matrix[cell, (cell - reach) % count] += weight
        return matrix

    def split(matrix):
        high = matrix.astype(ml_dtypes.bfloat16)
        low = (matrix - high.astype(np.float64)).astype(ml_dtypes.bfloat16)
        return high, low

    z_high, z_low = split(circulant(256))
    y_high, y_low = split(np.kron(np.eye(8), circulant(32)))
    x_high, x_low = split(np.kron(circulant(32), np.eye(8)))
    both = np.concatenate([y_high[:128, :128], y_high[:128, :128]], axis=1)
    return np.concatenate([z_high, z_low, x_high, x_low, y_low, both])


Z_HIGH, Z_LOW, X_HIGH, X_LOW, Y_LOW = (slice(i * 256, i * 256 + 256) for i in range(5))
Y_BOTH = slice(5 * 256, 5 * 256 + 128)


def dot(left, right):
    return jnp.dot(left, right, preferred_element_type=jnp.float32)


def split(field):
    high = field.astype(jnp.bfloat16)
    return high, (field - high.astype(jnp.float32)).astype(jnp.bfloat16)


def add_along_x(field_ref, mats, out_ref, start):
    for tile in range(4):
        ys = slice(tile * 8, tile * 8 + 8)
        if tile < 2:
            field = field_ref[:, ys, :]
            high, low = split(field.reshape(256, 256))
            shifts = dot(mats[X_HIGH], high) + dot(mats[X_HIGH], low) + dot(mats[X_LOW], high)
            out_ref[:, ys, :] = start(field, (slice(None), ys, slice(None))) + FIRST * shifts.reshape(
                32, 8, 256
            )
            continue
        for part in range(2):
            zs = slice(part * LANES, (part + 1) * LANES)
            planes = [field_ref[x, ys, zs] for x in range(32)]
            for x in range(32):
                total = start(planes[x], (x, ys, zs))
                for reach in range(1, 7):
                    pair = planes[(x + reach) % 32] + planes[(x - reach) % 32]
                    total = total + (STENCIL_WEIGHTS[reach] * KINETIC * STEP) * pair
                out_ref[x, ys, zs] = total


def along_yz(field_ref, mats, g):
    center = field_ref[g * 8 : g * 8 + 8]
    high, low = split(center.reshape(256, 256))
    shifts = dot(high, mats[Z_HIGH]) + dot(low, mats[Z_HIGH]) + dot(high, mats[Z_LOW])
    along_y = [
        dot(mats[Y_BOTH], jnp.concatenate([high[rows], low[rows]], axis=0))
        for rows in (slice(0, 128), slice(128, 256))
    ]
    shifts = shifts + jnp.concatenate(along_y, axis=0) + dot(mats[Y_LOW], high)
    return FIRST * shifts.reshape(8, 32, 256), center


def domain(gx, gy):
    return gx * 4 + gy, slice(gx * 8, gx * 8 + 8), slice(gy * 8, gy * 8 + 8)


def own_tile_kernel(recv_ref, out_ref):
    out_ref[...] = recv_ref[:, 2]


def kinetic_kernel(recv_ref, mats, field_ref, out_ref):
    for gx in range(4):
        for gy in range(4):
            src, xs, ys = domain(gx, gy)
            for part in range(2):
                zs = slice(part * LANES, (part + 1) * LANES)
                field_ref[xs, ys, zs] = recv_ref[src, part].reshape(8, 8, LANES)
    add_along_x(field_ref, mats, out_ref, lambda field, at: 0.0)
    for g in range(4):
        rows = slice(g * 8, g * 8 + 8)
        out_ref[rows] = 0.5 * (out_ref[rows] + along_yz(field_ref, mats, g)[0])


def filter_kernel(
    place_ref, recv_ref, other_ref, start_ref, first_ref, mats, out_ref, even_ref, odd_ref, pot_ref
):
    half, core = place_ref[0], place_ref[1]
    for gx in range(4):
        for gy in range(4):
            src, xs, ys = domain(gx, gy)
            mine = recv_ref[src, 2]
            theirs = other_ref[src]
            for part in range(2):
                zs = slice(part * LANES, (part + 1) * LANES)
                tile = jnp.where(core == part, mine, theirs).reshape(8, 8, LANES)
                local = (tile + (3.0 * STENCIL_WEIGHTS[0] * KINETIC - FILTER_CENTER)) * STEP
                pot_ref[xs, ys, zs] = local
                odd_ref[xs, ys, zs] = first_ref[xs, ys, zs] + 0.5 * local * start_ref[xs, ys, zs]

    for step in range(1, DEGREE):
        current, following = (odd_ref, even_ref) if step % 2 else (even_ref, odd_ref)
        previous = start_ref if step == 1 else following
        add_along_x(
            current,
            mats,
            following,
            lambda field, at, previous=previous: pot_ref[at] * field - previous[at],
        )
        for g in range(4):
            rows = slice(g * 8, g * 8 + 8)
            following[rows] = following[rows] + along_yz(current, mats, g)[0]

    last, spare = (odd_ref, even_ref) if DEGREE % 2 else (even_ref, odd_ref)
    add_along_x(last, mats, spare, lambda field, at: pot_ref[at] * field)
    own = (lax.broadcasted_iota(jnp.int32, (8, 4, 8, LANES), 3) < 64) == (half == 0)
    for g in range(4):
        shifts, center = along_yz(last, mats, g)
        total = spare[g * 8 : g * 8 + 8] + shifts
        applied = total * (1.0 / STEP) + FILTER_CENTER * center
        tiles = center.reshape(8, 4, 8, 256)
        applied_tiles = applied.reshape(8, 4, 8, 256)
        moved = pltpu.roll(applied_tiles[..., LANES:].reshape(256, LANES), 64, 1)
        out_ref[:, g, :, 0:8] = tiles[..., :LANES]
        out_ref[:, g, :, 8:16] = applied_tiles[..., :LANES]
        out_ref[:, g, :, 16:24] = jnp.where(
            own, tiles[..., LANES:], moved.reshape(8, 4, 8, LANES)
        )


def gram_kernel(recv_ref, out_ref):
    lane = lane_index(64)

    def rows_of(half, k):
        parts = [recv_ref[pl.ds((b * 2 + half) * 8 * 24 + k, 8, stride=24), :] for b in range(8)]
        return jnp.concatenate(parts, axis=0)

    def split(pieces):
        whole = jnp.concatenate(pieces, axis=1)
        high = whole.astype(jnp.bfloat16)
        low = (whole - high.astype(jnp.float32)).astype(jnp.bfloat16)
        return high, low

    total = jnp.zeros((128, 256), jnp.float32)
    for k in range(8):
        rest0, rest1 = rows_of(0, 16 + k), rows_of(1, 16 + k)
        rest = jnp.where(lane < 64, rest0, rest1)
        rest_applied = pltpu.roll(jnp.where(lane < 64, rest1, rest0), 64, 1)
        f1, f2 = split([rows_of(0, k), rows_of(1, k), rest])
        a1, a2 = split([rows_of(0, 8 + k), rows_of(1, 8 + k), rest_applied])
        total = total + lax.dot_general(
            jnp.concatenate([f1, f2], axis=0),
            jnp.concatenate([f1, a1, f2, a2], axis=0),
            (((1,), (1,)), ((), ())),
            preferred_element_type=jnp.float32,
        )
    total = total[:64] + total[64:]
    total = total[:, :LANES] + total[:, LANES:]
    near = lane_index(8) < 64
    for b in range(8):
        for j in range(8):
            zero, one = (((b * 2 + h) * 8 + j) * 24 for h in range(2))
            rest = jnp.where(near, recv_ref[zero + 16 : zero + 24], recv_ref[one + 16 : one + 24])
            out_ref[b, j * 8 : j * 8 + 8] = recv_ref[zero : zero + 8]
            out_ref[b, 64 + j * 8 : 64 + j * 8 + 8] = rest
            out_ref[b, 128 + j * 8 : 128 + j * 8 + 8] = recv_ref[one : one + 8]
        out_ref[b, 192:200] = total[b * 8 : b * 8 + 8]


def band_sum_kernel(recv_ref, out_ref):
    total = jnp.sum(recv_ref[:, 24], axis=0)
    out_ref[...] = jnp.broadcast_to(total[None], (16, 8, LANES))


def last_kernel(home_ref, sums_ref, out_ref, margin_ref, hamiltonian_ref, whole, rows, sems, *, scale):
    copies = []

    def send(source, target):
        copies.append(pltpu.make_async_copy(source, target, sems.at[len(copies)]))
        copies[-1].start()

    for j in range(8):
        for x in range(8):
            for part in range(3):
                zs = slice(part * LANES, (part + 1) * LANES)
                whole[j, x, :, zs] = home_ref[x, part * 8 + j]
        send(whole.at[j], out_ref.at[j])
        if j == 0:
            total = jnp.sum(sums_ref[...], axis=0) * scale
            rows[0] = total[:, :64]
            rows[1] = pltpu.roll(total, 64, 1)[:, :64]
            send(rows.at[0], margin_ref)
            send(rows.at[1], hamiltonian_ref)
    for copy in copies:
        copy.wait()


def call(kernel, shapes, *args, scratch=(), smem=0, keep=False):
    single = not isinstance(shapes, list)
    place = pltpu.VMEM if keep else jax.ShapeDtypeStruct
    outs = [place(s, jnp.float32) for s in ([shapes] if single else shapes)]
    specs = [pl.BlockSpec(memory_space=pltpu.SMEM)] * smem + [VMEM] * (len(args) - smem)
    result = pl.pallas_call(
        kernel,
        out_shape=outs[0] if single else outs,
        in_specs=specs,
        out_specs=VMEM if single else [VMEM] * len(outs),
        scratch_shapes=list(scratch),
        compiler_params=PARAMS,
    )(*args)
    return result


def exchange(array, axes):
    return lax.all_to_all(array, axes, split_axis=0, concat_axis=0, tiled=True)


def pack(orbitals, potential):
    matrices = jnp.asarray(band_matrices())
    args = (orbitals, potential, matrices)
    return pl.pallas_call(
        pack_kernel,
        out_shape=[
            pltpu.VMEM((2, 8, 3, 64, LANES), jnp.float32),
            pltpu.VMEM(matrices.shape, jnp.bfloat16),
        ],
        in_specs=[pl.BlockSpec(memory_space=pltpu.HBM)] * 3,
        out_specs=[VMEM] * 2,
        scratch_shapes=[
            pltpu.VMEM((8, 8, 8, 384), jnp.float32),
            pltpu.VMEM((8, 8, 384), jnp.float32),
            pltpu.SemaphoreType.DMA((10,)),
        ],
        compiler_params=PARAMS,
    )(*(pltpu.with_memory_space_constraint(a, pltpu.HBM) for a in args))


def per_device(orbitals, potential):
    packed, matrices = pack(orbitals, potential)
    windows = exchange(packed.reshape(16, 3, 64, LANES), GRID_AXES)
    mine = call(own_tile_kernel, (16, 64, LANES), windows, keep=True)
    other = lax.ppermute(mine, "gx", [(0, 1), (1, 0), (2, 3), (3, 2)])
    place = lax.axis_index("gx")
    place = jnp.stack([place // 2, place % 2]).astype(jnp.int32)
    whole = pltpu.VMEM((32, 32, 256), jnp.float32)
    start, first = call(
        kinetic_kernel, [(32, 32, 256), (32, 32, 256)], windows, matrices, keep=True
    )
    rows = call(
        filter_kernel,
        (8, 4, 4, 24, LANES),
        place,
        windows,
        other,
        start,
        first,
        matrices,
        scratch=(whole, whole, whole),
        smem=1,
    )
    cells = exchange(rows.reshape(128, 24, LANES), ALL_AXES)
    outgoing = call(gram_kernel, (8, 200, LANES), cells.reshape(128 * 24, LANES))
    home = exchange(outgoing, "band").reshape(8, 25, 8, LANES)
    sums = exchange(call(band_sum_kernel, (16, 8, LANES), home, keep=True), GRID_AXES)
    return pl.pallas_call(
        functools.partial(last_kernel, scale=1.0 / (8 * 8 * 384)),
        out_shape=[
            pltpu.HBM((8, 8, 8, 384), jnp.float32),
            pltpu.HBM((8, 64), jnp.float32),
            pltpu.HBM((8, 64), jnp.float32),
        ],
        in_specs=[VMEM] * 2,
        out_specs=[pl.BlockSpec(memory_space=pltpu.HBM)] * 3,
        scratch_shapes=[
            pltpu.VMEM((8, 8, 8, 384), jnp.float32),
            pltpu.VMEM((2, 8, 64), jnp.float32),
            pltpu.SemaphoreType.DMA((10,)),
        ],
        compiler_params=PARAMS,
    )(home, sums)


def solution(mesh):
    placed = (P("band", "gx", "gy", None), P("gx", "gy", None))
    return jax.shard_map(
        per_device,
        mesh=mesh,
        in_specs=placed,
        out_specs=(P("band", "gx", "gy", None), P("band", None), P("band", None)),
        check_vma=False,
    )
```

```python
import functools

import jax
import jax.numpy as jnp
import ml_dtypes
import numpy as np
from jax import lax
from jax.experimental import pallas as pl
from jax.experimental.pallas import tpu as pltpu
from jax.sharding import PartitionSpec as P

DEGREE = 4

STENCIL_WEIGHTS = (
    -5369.0 / 1800.0,
    12.0 / 7.0,
    -15.0 / 56.0,
    10.0 / 189.0,
    -1.0 / 112.0,
    2.0 / 1925.0,
    -1.0 / 16632.0,
)
GRID_SPACING = 0.5
FILTER_CENTER = 24.0
FILTER_HALFWIDTH = 20.0
KINETIC = -0.5 / (GRID_SPACING * GRID_SPACING)
STEP = 2.0 / FILTER_HALFWIDTH
FIRST = STENCIL_WEIGHTS[1] * KINETIC * STEP
GRID_AXES = ("gx", "gy")
ALL_AXES = ("band", "gx", "gy")
LANES = 128
VMEM = pl.BlockSpec(memory_space=pltpu.VMEM)
PARAMS = pltpu.CompilerParams(vmem_limit_bytes=24 * 1024 * 1024)


def lane_index(rows):
    return lax.broadcasted_iota(jnp.int32, (rows, LANES), 1)


def pack_kernel(orb_ref, pot_ref, mats_ref, out_ref, mats_out_ref, orb, pot, sems):
    loads = [pltpu.make_async_copy(pot_ref, pot, sems.at[8])]
    loads += [pltpu.make_async_copy(orb_ref.at[j], orb.at[j], sems.at[j]) for j in range(8)]
    loads += [pltpu.make_async_copy(mats_ref, mats_out_ref, sems.at[9])]
    for load in loads:
        load.start()
    lane = lane_index(64)

    def windows(block):
        z0, z1, z2 = (block[:, :, i * LANES : (i + 1) * LANES].reshape(64, LANES) for i in range(3))
        return (
            (z0, jnp.where(lane < 96, z1, z2)),
            (z2, jnp.where(lane < 32, z0, z1)),
        )

    loads[0].wait()
    pot_windows = windows(pot[...])
    for half in range(2):
        for j in range(8):
            out_ref[half, j, 2] = pot_windows[half][j // 4]
    for j in range(8):
        loads[1 + j].wait()
        orb_windows = windows(orb[j])
        for half in range(2):
            for part in range(2):
                out_ref[half, j, part] = orb_windows[half][part]
    loads[9].wait()


def band_matrices():
    def circulant(count):
        matrix = np.zeros((count, count), np.float64)
        for reach in range(1, 7):
            for cell in range(count):
                weight = STENCIL_WEIGHTS[reach] / STENCIL_WEIGHTS[1]
                matrix[cell, (cell + reach) % count] += weight
                matrix[cell, (cell - reach) % count] += weight
        return matrix

    def split(matrix):
        high = matrix.astype(ml_dtypes.bfloat16)
        low = (matrix - high.astype(np.float64)).astype(ml_dtypes.bfloat16)
        return high, low

    z_high, z_low = split(circulant(256))
    y_high, y_low = split(np.kron(np.eye(8), circulant(32)))
    x_high, x_low = split(np.kron(circulant(32), np.eye(8)))
    both = np.concatenate([y_high[:128, :128], y_high[:128, :128]], axis=1)
    return np.concatenate([z_high, z_low, x_high, x_low, y_low, both])


Z_HIGH, Z_LOW, X_HIGH, X_LOW, Y_LOW = (slice(i * 256, i * 256 + 256) for i in range(5))
Y_BOTH = slice(5 * 256, 5 * 256 + 128)


def dot(left, right):
    return jnp.dot(left, right, preferred_element_type=jnp.float32)


def split(field):
    high = field.astype(jnp.bfloat16)
    return high, (field - high.astype(jnp.float32)).astype(jnp.bfloat16)


def add_along_x(field_ref, mats, out_ref, start):
    for tile in range(4):
        ys = slice(tile * 8, tile * 8 + 8)
        if tile < 2:
            field = field_ref[:, ys, :]
            high, low = split(field.reshape(256, 256))
            shifts = dot(mats[X_HIGH], high) + dot(mats[X_HIGH], low) + dot(mats[X_LOW], high)
            out_ref[:, ys, :] = start(field, (slice(None), ys, slice(None))) + FIRST * shifts.reshape(
                32, 8, 256
            )
            continue
        for part in range(2):
            zs = slice(part * LANES, (part + 1) * LANES)
            planes = [field_ref[x, ys, zs] for x in range(32)]
            for x in range(32):
                total = start(planes[x], (x, ys, zs))
                for reach in range(1, 7):
                    pair = planes[(x + reach) % 32] + planes[(x - reach) % 32]
                    total = total + (STENCIL_WEIGHTS[reach] * KINETIC * STEP) * pair
                out_ref[x, ys, zs] = total


def along_yz(field_ref, mats, g):
    center = field_ref[g * 8 : g * 8 + 8]
    high, low = split(center.reshape(256, 256))
    shifts = dot(high, mats[Z_HIGH]) + dot(low, mats[Z_HIGH]) + dot(high, mats[Z_LOW])
    along_y = [
        dot(mats[Y_BOTH], jnp.concatenate([high[rows], low[rows]], axis=0))
        for rows in (slice(0, 128), slice(128, 256))
    ]
    shifts = shifts + jnp.concatenate(along_y, axis=0) + dot(mats[Y_LOW], high)
    return FIRST * shifts.reshape(8, 32, 256), center


def domain(gx, gy):
    return gx * 4 + gy, slice(gx * 8, gx * 8 + 8), slice(gy * 8, gy * 8 + 8)


def own_tile_kernel(recv_ref, out_ref):
    out_ref[...] = recv_ref[:, 2]


def kinetic_kernel(recv_ref, mats, field_ref, out_ref):
    for gx in range(4):
        for gy in range(4):
            src, xs, ys = domain(gx, gy)
            for part in range(2):
                zs = slice(part * LANES, (part + 1) * LANES)
                field_ref[xs, ys, zs] = recv_ref[src, part].reshape(8, 8, LANES)
    add_along_x(field_ref, mats, out_ref, lambda field, at: 0.0)
    for g in range(4):
        rows = slice(g * 8, g * 8 + 8)
        out_ref[rows] = 0.5 * (out_ref[rows] + along_yz(field_ref, mats, g)[0])


def filter_kernel(
    recv_ref, other_ref, start_ref, first_ref, mats, out_ref, even_ref, odd_ref, pot_ref
):
    place = lax.axis_index("gx")
    half, core = place // 2, place % 2
    for gx in range(4):
        for gy in range(4):
            src, xs, ys = domain(gx, gy)
            mine = recv_ref[src, 2]
            theirs = other_ref[src]
            for part in range(2):
                zs = slice(part * LANES, (part + 1) * LANES)
                tile = jnp.where(core == part, mine, theirs).reshape(8, 8, LANES)
                local = (tile + (3.0 * STENCIL_WEIGHTS[0] * KINETIC - FILTER_CENTER)) * STEP
                pot_ref[xs, ys, zs] = local
                odd_ref[xs, ys, zs] = first_ref[xs, ys, zs] + 0.5 * local * start_ref[xs, ys, zs]

    for step in range(1, DEGREE):
        current, following = (odd_ref, even_ref) if step % 2 else (even_ref, odd_ref)
        previous = start_ref if step == 1 else following
        add_along_x(
            current,
            mats,
            following,
            lambda field, at, previous=previous: pot_ref[at] * field - previous[at],
        )
        for g in range(4):
            rows = slice(g * 8, g * 8 + 8)
            following[rows] = following[rows] + along_yz(current, mats, g)[0]

    last, spare = (odd_ref, even_ref) if DEGREE % 2 else (even_ref, odd_ref)
    add_along_x(last, mats, spare, lambda field, at: pot_ref[at] * field)
    own = (lax.broadcasted_iota(jnp.int32, (8, 4, 8, LANES), 3) < 64) == (half == 0)
    for g in range(4):
        shifts, center = along_yz(last, mats, g)
        total = spare[g * 8 : g * 8 + 8] + shifts
        applied = total * (1.0 / STEP) + FILTER_CENTER * center
        tiles = center.reshape(8, 4, 8, 256)
        applied_tiles = applied.reshape(8, 4, 8, 256)
        moved = pltpu.roll(applied_tiles[..., LANES:].reshape(256, LANES), 64, 1)
        out_ref[:, g, :, 0:8] = tiles[..., :LANES]
        out_ref[:, g, :, 8:16] = applied_tiles[..., :LANES]
        out_ref[:, g, :, 16:24] = jnp.where(
            own, tiles[..., LANES:], moved.reshape(8, 4, 8, LANES)
        )


def gram_kernel(recv_ref, out_ref):
    lane = lane_index(64)

    def rows_of(half, k):
        parts = [recv_ref[pl.ds((b * 2 + half) * 8 * 24 + k, 8, stride=24), :] for b in range(8)]
        return jnp.concatenate(parts, axis=0)

    def split(pieces):
        whole = jnp.concatenate(pieces, axis=1)
        high = whole.astype(jnp.bfloat16)
        low = (whole - high.astype(jnp.float32)).astype(jnp.bfloat16)
        return high, low

    total = jnp.zeros((128, 256), jnp.float32)
    for k in range(8):
        rest0, rest1 = rows_of(0, 16 + k), rows_of(1, 16 + k)
        rest = jnp.where(lane < 64, rest0, rest1)
        rest_applied = pltpu.roll(jnp.where(lane < 64, rest1, rest0), 64, 1)
        f1, f2 = split([rows_of(0, k), rows_of(1, k), rest])
        a1, a2 = split([rows_of(0, 8 + k), rows_of(1, 8 + k), rest_applied])
        total = total + lax.dot_general(
            jnp.concatenate([f1, f2], axis=0),
            jnp.concatenate([f1, a1, f2, a2], axis=0),
            (((1,), (1,)), ((), ())),
            preferred_element_type=jnp.float32,
        )
    total = total[:64] + total[64:]
    total = total[:, :LANES] + total[:, LANES:]
    near = lane_index(8) < 64
    for b in range(8):
        for j in range(8):
            zero, one = (((b * 2 + h) * 8 + j) * 24 for h in range(2))
            rest = jnp.where(near, recv_ref[zero + 16 : zero + 24], recv_ref[one + 16 : one + 24])
            out_ref[b, j * 8 : j * 8 + 8] = recv_ref[zero : zero + 8]
            out_ref[b, 64 + j * 8 : 64 + j * 8 + 8] = rest
            out_ref[b, 128 + j * 8 : 128 + j * 8 + 8] = recv_ref[one : one + 8]
        out_ref[b, 192:200] = total[b * 8 : b * 8 + 8]


def band_sum_kernel(recv_ref, out_ref):
    total = jnp.sum(recv_ref[:, 24], axis=0)
    out_ref[...] = jnp.broadcast_to(total[None], (16, 8, LANES))


def last_kernel(home_ref, sums_ref, out_ref, margin_ref, hamiltonian_ref, whole, rows, sems, *, scale):
    copies = []

    def send(source, target):
        copies.append(pltpu.make_async_copy(source, target, sems.at[len(copies)]))
        copies[-1].start()

    for j in range(8):
        for x in range(8):
            for part in range(3):
                zs = slice(part * LANES, (part + 1) * LANES)
                whole[j, x, :, zs] = home_ref[x, part * 8 + j]
        send(whole.at[j], out_ref.at[j])
        if j == 0:
            total = jnp.sum(sums_ref[...], axis=0) * scale
            rows[0] = total[:, :64]
            rows[1] = pltpu.roll(total, 64, 1)[:, :64]
            send(rows.at[0], margin_ref)
            send(rows.at[1], hamiltonian_ref)
    for copy in copies:
        copy.wait()


def call(kernel, shapes, *args, scratch=(), keep=False):
    single = not isinstance(shapes, list)
    place = pltpu.VMEM if keep else jax.ShapeDtypeStruct
    outs = [place(s, jnp.float32) for s in ([shapes] if single else shapes)]
    specs = [VMEM] * len(args)
    result = pl.pallas_call(
        kernel,
        out_shape=outs[0] if single else outs,
        in_specs=specs,
        out_specs=VMEM if single else [VMEM] * len(outs),
        scratch_shapes=list(scratch),
        compiler_params=PARAMS,
    )(*args)
    return result


def exchange(array, axes):
    return lax.all_to_all(array, axes, split_axis=0, concat_axis=0, tiled=True)


def pack(orbitals, potential):
    matrices = jnp.asarray(band_matrices())
    args = (orbitals, potential, matrices)
    return pl.pallas_call(
        pack_kernel,
        out_shape=[
            pltpu.VMEM((2, 8, 3, 64, LANES), jnp.float32),
            pltpu.VMEM(matrices.shape, jnp.bfloat16),
        ],
        in_specs=[pl.BlockSpec(memory_space=pltpu.HBM)] * 3,
        out_specs=[VMEM] * 2,
        scratch_shapes=[
            pltpu.VMEM((8, 8, 8, 384), jnp.float32),
            pltpu.VMEM((8, 8, 384), jnp.float32),
            pltpu.SemaphoreType.DMA((10,)),
        ],
        compiler_params=PARAMS,
    )(*(pltpu.with_memory_space_constraint(a, pltpu.HBM) for a in args))


def per_device(orbitals, potential):
    packed, matrices = pack(orbitals, potential)
    windows = exchange(packed.reshape(16, 3, 64, LANES), GRID_AXES)
    mine = call(own_tile_kernel, (16, 64, LANES), windows, keep=True)
    other = lax.ppermute(mine, "gx", [(0, 1), (1, 0), (2, 3), (3, 2)])
    whole = pltpu.VMEM((32, 32, 256), jnp.float32)
    start, first = call(
        kinetic_kernel, [(32, 32, 256), (32, 32, 256)], windows, matrices, keep=True
    )
    rows = call(
        filter_kernel,
        (8, 4, 4, 24, LANES),
        windows,
        other,
        start,
        first,
        matrices,
        scratch=(whole, whole, whole),
    )
    cells = exchange(rows.reshape(128, 24, LANES), ALL_AXES)
    outgoing = call(gram_kernel, (8, 200, LANES), cells.reshape(128 * 24, LANES))
    home = exchange(outgoing, "band").reshape(8, 25, 8, LANES)
    sums = exchange(call(band_sum_kernel, (16, 8, LANES), home, keep=True), GRID_AXES)
    return pl.pallas_call(
        functools.partial(last_kernel, scale=1.0 / (8 * 8 * 384)),
        out_shape=[
            pltpu.HBM((8, 8, 8, 384), jnp.float32),
            pltpu.HBM((8, 64), jnp.float32),
            pltpu.HBM((8, 64), jnp.float32),
        ],
        in_specs=[VMEM] * 2,
        out_specs=[pl.BlockSpec(memory_space=pltpu.HBM)] * 3,
        scratch_shapes=[
            pltpu.VMEM((8, 8, 8, 384), jnp.float32),
            pltpu.VMEM((2, 8, 64), jnp.float32),
            pltpu.SemaphoreType.DMA((10,)),
        ],
        compiler_params=PARAMS,
    )(home, sums)


def solution(mesh):
    placed = (P("band", "gx", "gy", None), P("gx", "gy", None))
    return jax.shard_map(
        per_device,
        mesh=mesh,
        in_specs=placed,
        out_specs=(P("band", "gx", "gy", None), P("band", None), P("band", None)),
        check_vma=False,
    )
```

```python
import functools

import jax
import jax.numpy as jnp
import ml_dtypes
import numpy as np
from jax import lax
from jax.experimental import pallas as pl
from jax.experimental.pallas import tpu as pltpu
from jax.sharding import PartitionSpec as P

DEGREE = 4

STENCIL_WEIGHTS = (
    -5369.0 / 1800.0,
    12.0 / 7.0,
    -15.0 / 56.0,
    10.0 / 189.0,
    -1.0 / 112.0,
    2.0 / 1925.0,
    -1.0 / 16632.0,
)
GRID_SPACING = 0.5
FILTER_CENTER = 24.0
FILTER_HALFWIDTH = 20.0
KINETIC = -0.5 / (GRID_SPACING * GRID_SPACING)
STEP = 2.0 / FILTER_HALFWIDTH
FIRST = STENCIL_WEIGHTS[1] * KINETIC * STEP
GRID_AXES = ("gx", "gy")
ALL_AXES = ("band", "gx", "gy")
LANES = 128
VMEM = pl.BlockSpec(memory_space=pltpu.VMEM)
PARAMS = pltpu.CompilerParams(vmem_limit_bytes=24 * 1024 * 1024)


def lane_index(rows):
    return lax.broadcasted_iota(jnp.int32, (rows, LANES), 1)


def pack_kernel(orb_ref, pot_ref, mats_ref, out_ref, mats_out_ref, orb, pot, sems):
    loads = [pltpu.make_async_copy(pot_ref, pot, sems.at[8])]
    loads += [pltpu.make_async_copy(orb_ref.at[j], orb.at[j], sems.at[j]) for j in range(8)]
    loads += [pltpu.make_async_copy(mats_ref, mats_out_ref, sems.at[9])]
    for load in loads[1:9] + [loads[0], loads[9]]:
        load.start()
    lane = lane_index(64)

    def windows(block):
        z0, z1, z2 = (block[:, :, i * LANES : (i + 1) * LANES].reshape(64, LANES) for i in range(3))
        return (
            (z0, jnp.where(lane < 96, z1, z2)),
            (z2, jnp.where(lane < 32, z0, z1)),
        )

    for j in range(8):
        loads[1 + j].wait()
        orb_windows = windows(orb[j])
        for half in range(2):
            for part in range(2):
                out_ref[half, j, part] = orb_windows[half][part]
    loads[0].wait()
    pot_windows = windows(pot[...])
    for half in range(2):
        for j in range(8):
            out_ref[half, j, 2] = pot_windows[half][j // 4]
    loads[9].wait()


def band_matrices():
    def circulant(count):
        matrix = np.zeros((count, count), np.float64)
        for reach in range(1, 7):
            for cell in range(count):
                weight = STENCIL_WEIGHTS[reach] / STENCIL_WEIGHTS[1]
                matrix[cell, (cell + reach) % count] += weight
                matrix[cell, (cell - reach) % count] += weight
        return matrix

    def split(matrix):
        high = matrix.astype(ml_dtypes.bfloat16)
        low = (matrix - high.astype(np.float64)).astype(ml_dtypes.bfloat16)
        return high, low

    z_high, z_low = split(circulant(256))
    y_high, y_low = split(np.kron(np.eye(8), circulant(32)))
    x_high, x_low = split(np.kron(circulant(32), np.eye(8)))
    both = np.concatenate([y_high[:128, :128], y_high[:128, :128]], axis=1)
    return np.concatenate([z_high, z_low, x_high, x_low, y_low, both])


Z_HIGH, Z_LOW, X_HIGH, X_LOW, Y_LOW = (slice(i * 256, i * 256 + 256) for i in range(5))
Y_BOTH = slice(5 * 256, 5 * 256 + 128)


def dot(left, right):
    return jnp.dot(left, right, preferred_element_type=jnp.float32)


def split(field):
    high = field.astype(jnp.bfloat16)
    return high, (field - high.astype(jnp.float32)).astype(jnp.bfloat16)


def add_along_x(field_ref, mats, out_ref, start):
    for tile in range(4):
        ys = slice(tile * 8, tile * 8 + 8)
        if tile < 2:
            field = field_ref[:, ys, :]
            high, low = split(field.reshape(256, 256))
            shifts = dot(mats[X_HIGH], high) + dot(mats[X_HIGH], low) + dot(mats[X_LOW], high)
            out_ref[:, ys, :] = start(field, (slice(None), ys, slice(None))) + FIRST * shifts.reshape(
                32, 8, 256
            )
            continue
        for part in range(2):
            zs = slice(part * LANES, (part + 1) * LANES)
            planes = [field_ref[x, ys, zs] for x in range(32)]
            for x in range(32):
                total = start(planes[x], (x, ys, zs))
                for reach in range(1, 7):
                    pair = planes[(x + reach) % 32] + planes[(x - reach) % 32]
                    total = total + (STENCIL_WEIGHTS[reach] * KINETIC * STEP) * pair
                out_ref[x, ys, zs] = total


def along_yz(field_ref, mats, g):
    center = field_ref[g * 8 : g * 8 + 8]
    high, low = split(center.reshape(256, 256))
    shifts = dot(high, mats[Z_HIGH]) + dot(low, mats[Z_HIGH]) + dot(high, mats[Z_LOW])
    along_y = [
        dot(mats[Y_BOTH], jnp.concatenate([high[rows], low[rows]], axis=0))
        for rows in (slice(0, 128), slice(128, 256))
    ]
    shifts = shifts + jnp.concatenate(along_y, axis=0) + dot(mats[Y_LOW], high)
    return FIRST * shifts.reshape(8, 32, 256), center


def domain(gx, gy):
    return gx * 4 + gy, slice(gx * 8, gx * 8 + 8), slice(gy * 8, gy * 8 + 8)


def own_tile_kernel(recv_ref, out_ref):
    out_ref[...] = recv_ref[:, 2]


def kinetic_kernel(recv_ref, mats, field_ref, out_ref):
    for gx in range(4):
        for gy in range(4):
            src, xs, ys = domain(gx, gy)
            for part in range(2):
                zs = slice(part * LANES, (part + 1) * LANES)
                field_ref[xs, ys, zs] = recv_ref[src, part].reshape(8, 8, LANES)
    add_along_x(field_ref, mats, out_ref, lambda field, at: 0.0)
    for g in range(4):
        rows = slice(g * 8, g * 8 + 8)
        out_ref[rows] = 0.5 * (out_ref[rows] + along_yz(field_ref, mats, g)[0])


def filter_kernel(
    recv_ref, other_ref, start_ref, first_ref, mats, out_ref, even_ref, odd_ref, pot_ref
):
    place = lax.axis_index("gx")
    half, core = place // 2, place % 2
    for gx in range(4):
        for gy in range(4):
            src, xs, ys = domain(gx, gy)
            mine = recv_ref[src, 2]
            theirs = other_ref[src]
            for part in range(2):
                zs = slice(part * LANES, (part + 1) * LANES)
                tile = jnp.where(core == part, mine, theirs).reshape(8, 8, LANES)
                local = (tile + (3.0 * STENCIL_WEIGHTS[0] * KINETIC - FILTER_CENTER)) * STEP
                pot_ref[xs, ys, zs] = local
                odd_ref[xs, ys, zs] = first_ref[xs, ys, zs] + 0.5 * local * start_ref[xs, ys, zs]

    for step in range(1, DEGREE):
        current, following = (odd_ref, even_ref) if step % 2 else (even_ref, odd_ref)
        previous = start_ref if step == 1 else following
        add_along_x(
            current,
            mats,
            following,
            lambda field, at, previous=previous: pot_ref[at] * field - previous[at],
        )
        for g in range(4):
            rows = slice(g * 8, g * 8 + 8)
            following[rows] = following[rows] + along_yz(current, mats, g)[0]

    last, spare = (odd_ref, even_ref) if DEGREE % 2 else (even_ref, odd_ref)
    add_along_x(last, mats, spare, lambda field, at: pot_ref[at] * field)
    own = (lax.broadcasted_iota(jnp.int32, (8, 4, 8, LANES), 3) < 64) == (half == 0)
    for g in range(4):
        shifts, center = along_yz(last, mats, g)
        total = spare[g * 8 : g * 8 + 8] + shifts
        applied = total * (1.0 / STEP) + FILTER_CENTER * center
        tiles = center.reshape(8, 4, 8, 256)
        applied_tiles = applied.reshape(8, 4, 8, 256)
        moved = pltpu.roll(applied_tiles[..., LANES:].reshape(256, LANES), 64, 1)
        out_ref[:, g, :, 0:8] = tiles[..., :LANES]
        out_ref[:, g, :, 8:16] = applied_tiles[..., :LANES]
        out_ref[:, g, :, 16:24] = jnp.where(
            own, tiles[..., LANES:], moved.reshape(8, 4, 8, LANES)
        )


def gram_kernel(recv_ref, out_ref):
    lane = lane_index(64)

    def rows_of(half, k):
        parts = [recv_ref[pl.ds((b * 2 + half) * 8 * 24 + k, 8, stride=24), :] for b in range(8)]
        return jnp.concatenate(parts, axis=0)

    def split(pieces):
        whole = jnp.concatenate(pieces, axis=1)
        high = whole.astype(jnp.bfloat16)
        low = (whole - high.astype(jnp.float32)).astype(jnp.bfloat16)
        return high, low

    total = jnp.zeros((128, 256), jnp.float32)
    for k in range(8):
        rest0, rest1 = rows_of(0, 16 + k), rows_of(1, 16 + k)
        rest = jnp.where(lane < 64, rest0, rest1)
        rest_applied = pltpu.roll(jnp.where(lane < 64, rest1, rest0), 64, 1)
        f1, f2 = split([rows_of(0, k), rows_of(1, k), rest])
        a1, a2 = split([rows_of(0, 8 + k), rows_of(1, 8 + k), rest_applied])
        total = total + lax.dot_general(
            jnp.concatenate([f1, f2], axis=0),
            jnp.concatenate([f1, a1, f2, a2], axis=0),
            (((1,), (1,)), ((), ())),
            preferred_element_type=jnp.float32,
        )
    total = total[:64] + total[64:]
    total = total[:, :LANES] + total[:, LANES:]
    near = lane_index(8) < 64
    for b in range(8):
        for j in range(8):
            zero, one = (((b * 2 + h) * 8 + j) * 24 for h in range(2))
            rest = jnp.where(near, recv_ref[zero + 16 : zero + 24], recv_ref[one + 16 : one + 24])
            out_ref[b, j * 8 : j * 8 + 8] = recv_ref[zero : zero + 8]
            out_ref[b, 64 + j * 8 : 64 + j * 8 + 8] = rest
            out_ref[b, 128 + j * 8 : 128 + j * 8 + 8] = recv_ref[one : one + 8]
        out_ref[b, 192:200] = total[b * 8 : b * 8 + 8]


def band_sum_kernel(recv_ref, out_ref):
    total = jnp.sum(recv_ref[:, 24], axis=0)
    out_ref[...] = jnp.broadcast_to(total[None], (16, 8, LANES))


def last_kernel(home_ref, sums_ref, out_ref, margin_ref, hamiltonian_ref, whole, rows, sems, *, scale):
    copies = []

    def send(source, target):
        copies.append(pltpu.make_async_copy(source, target, sems.at[len(copies)]))
        copies[-1].start()

    for j in range(8):
        for x in range(8):
            for part in range(3):
                zs = slice(part * LANES, (part + 1) * LANES)
                whole[j, x, :, zs] = home_ref[x, part * 8 + j]
        send(whole.at[j], out_ref.at[j])
        if j == 0:
            total = jnp.sum(sums_ref[...], axis=0) * scale
            rows[0] = total[:, :64]
            rows[1] = pltpu.roll(total, 64, 1)[:, :64]
            send(rows.at[0], margin_ref)
            send(rows.at[1], hamiltonian_ref)
    for copy in copies:
        copy.wait()


def call(kernel, shapes, *args, scratch=(), keep=False):
    single = not isinstance(shapes, list)
    place = pltpu.VMEM if keep else jax.ShapeDtypeStruct
    outs = [place(s, jnp.float32) for s in ([shapes] if single else shapes)]
    specs = [VMEM] * len(args)
    result = pl.pallas_call(
        kernel,
        out_shape=outs[0] if single else outs,
        in_specs=specs,
        out_specs=VMEM if single else [VMEM] * len(outs),
        scratch_shapes=list(scratch),
        compiler_params=PARAMS,
    )(*args)
    return result


def exchange(array, axes):
    return lax.all_to_all(array, axes, split_axis=0, concat_axis=0, tiled=True)


def pack(orbitals, potential):
    matrices = jnp.asarray(band_matrices())
    args = (orbitals, potential, matrices)
    return pl.pallas_call(
        pack_kernel,
        out_shape=[
            pltpu.VMEM((2, 8, 3, 64, LANES), jnp.float32),
            pltpu.VMEM(matrices.shape, jnp.bfloat16),
        ],
        in_specs=[pl.BlockSpec(memory_space=pltpu.HBM)] * 3,
        out_specs=[VMEM] * 2,
        scratch_shapes=[
            pltpu.VMEM((8, 8, 8, 384), jnp.float32),
            pltpu.VMEM((8, 8, 384), jnp.float32),
            pltpu.SemaphoreType.DMA((10,)),
        ],
        compiler_params=PARAMS,
    )(*(pltpu.with_memory_space_constraint(a, pltpu.HBM) for a in args))


def per_device(orbitals, potential):
    packed, matrices = pack(orbitals, potential)
    windows = exchange(packed.reshape(16, 3, 64, LANES), GRID_AXES)
    mine = call(own_tile_kernel, (16, 64, LANES), windows, keep=True)
    other = lax.ppermute(mine, "gx", [(0, 1), (1, 0), (2, 3), (3, 2)])
    whole = pltpu.VMEM((32, 32, 256), jnp.float32)
    start, first = call(
        kinetic_kernel, [(32, 32, 256), (32, 32, 256)], windows, matrices, keep=True
    )
    rows = call(
        filter_kernel,
        (8, 4, 4, 24, LANES),
        windows,
        other,
        start,
        first,
        matrices,
        scratch=(whole, whole, whole),
    )
    cells = exchange(rows.reshape(128, 24, LANES), ALL_AXES)
    outgoing = call(gram_kernel, (8, 200, LANES), cells.reshape(128 * 24, LANES))
    home = exchange(outgoing, "band").reshape(8, 25, 8, LANES)
    sums = exchange(call(band_sum_kernel, (16, 8, LANES), home, keep=True), GRID_AXES)
    return pl.pallas_call(
        functools.partial(last_kernel, scale=1.0 / (8 * 8 * 384)),
        out_shape=[
            pltpu.HBM((8, 8, 8, 384), jnp.float32),
            pltpu.HBM((8, 64), jnp.float32),
            pltpu.HBM((8, 64), jnp.float32),
        ],
        in_specs=[VMEM] * 2,
        out_specs=[pl.BlockSpec(memory_space=pltpu.HBM)] * 3,
        scratch_shapes=[
            pltpu.VMEM((8, 8, 8, 384), jnp.float32),
            pltpu.VMEM((2, 8, 64), jnp.float32),
            pltpu.SemaphoreType.DMA((10,)),
        ],
        compiler_params=PARAMS,
    )(home, sums)


def solution(mesh):
    placed = (P("band", "gx", "gy", None), P("gx", "gy", None))
    return jax.shard_map(
        per_device,
        mesh=mesh,
        in_specs=placed,
        out_specs=(P("band", "gx", "gy", None), P("band", None), P("band", None)),
        check_vma=False,
    )
```
